512 devices in a mesh: dp: 64 (over z, y), mp: 8 (over x, core).
Axes of the slice: x: 4, y: 8, z: 8, core: 2. Of those that a mesh axis runs over, the one named last changes fastest.
Arguments:
- old_weight: float32 [24576, 3584], P('dp', 'mp'), may hold values from -6 to 6
- old_first: float32 [24576, 3584], P('dp', 'mp'), may hold values from -6 to 6
- old_second: float32 [24576, 3584], P('dp', 'mp'), may hold values from 0.1 to 3
- old_offsets: int32 [25], replicated, may hold values from 0 to 8192, as said below
- activations: bfloat16 [8192, 8192], P(('dp', 'mp')), may hold values from -6 to 6
- upstream: bfloat16 [8192, 3584], P('dp', 'mp'), may hold values from -0.0625 to 0.0625
Outputs:
- new_weight: float32 [8192, 3584], P('dp', 'mp')
- new_first: float32 [8192, 3584], P('dp', 'mp')
- new_second: float32 [8192, 3584], P('dp', 'mp')
- act_grad: bfloat16 [8192, 8192], P('mp', 'dp')
The draws below stay inside these ranges and needn't reach their ends.
Inputs may be any that keep to these rules, and one draw needn't show every extreme that they name: old_offsets rises from 0 to 8192; shard k holds rows old_offsets[k] to old_offsets[k+1] - 1 in the slots of dp index k; each shard has at most 384 rows, and one has exactly 384.
All inputs are finite; a program needn't handle non-finite values.
Results may differ from the reference program's by a relative error of at most 0.0049.
Values may be sent and summed in bfloat16 or wider, within the bound.
No kernel may reach another device: no remote copies, remote signals or barrier semaphores. Data moves between devices by JAX's collectives and lax.ppermute only.
A program may use at most 64 MiB of HBM per device.

```python
import math
import jax
import jax.numpy as jnp
from jax import lax

D = 8192
COLS = 3584
STEP = 24
TOKENS = 8192
OLD_SHARDS = 24
OLD_CAP = 384
N_DP = 64


def draw_old_offsets(key, part):
    key = jax.random.fold_in(key, 7)
    first_key, second_key = jax.random.split(key)
    others = OLD_SHARDS - 1
    remaining = D - OLD_CAP
    common = remaining // others
    leftover = remaining % others
    position = jnp.arange(others, dtype=jnp.int32)
    lengths = common + (position < leftover).astype(jnp.int32)
    spread = OLD_CAP - common - 1
    paired = jax.random.randint(first_key, (others // 2 + 1,), -spread, spread + 1, dtype=jnp.int32)
    moved = paired[position // 2] * (1 - 2 * (position % 2))
    lonely = jnp.logical_and(others % 2 == 1, position == others - 1)
    moved = jnp.where(lonely, 0, moved)
    lengths = (lengths + moved).astype(jnp.int32)
    lengths = jnp.concatenate([jnp.full((1,), OLD_CAP, jnp.int32), lengths])
    shuffle = jax.random.permutation(second_key, OLD_SHARDS)
    lengths = lengths[shuffle]
    return jnp.concatenate([jnp.zeros((1,), jnp.int32), jnp.cumsum(lengths).astype(jnp.int32)])


def shard_levels(rng, extent, shards, smallest, top_value):
    gain, own = 1.0, jax.random.fold_in(rng, 6)
    for axis_at, blocks in shards:
        heights = jnp.exp(jax.random.uniform(jax.random.fold_in(own, axis_at), (blocks,), jnp.float32, smallest / len(shards), top_value / len(shards)))
        gain = gain * jnp.repeat(heights, extent[axis_at] // blocks).reshape([-1 if axis == axis_at else 1 for axis in range(len(extent))])
    return gain


def centred(rng, shape, scale, limit, cuts=(), kind=jnp.bfloat16):
    loudness = shard_levels(rng, shape, cuts, -0.22, 0.18) if cuts else 1.0
    entries = jax.random.normal(rng, shape, jnp.float32) * scale * loudness
    return jnp.minimum(jnp.maximum(entries, -limit), limit).astype(kind)


def setup_inputs(seed: int = 0) -> dict:
    arg_keys = jax.random.split(jax.random.key(seed), 7)
    return {
        "old_weight": centred(arg_keys[0], (N_DP * OLD_CAP, COLS), 1.0, 6.0, ((0, 64), (1, 8)), jnp.float32),
        "old_first": centred(arg_keys[1], (N_DP * OLD_CAP, COLS), 1.0, 6.0, ((0, 64), (1, 8)), jnp.float32),
        "old_second": jnp.clip(jnp.exp(math.log(3.0) - 3.4011974 * jax.random.uniform(arg_keys[2], (N_DP * OLD_CAP, COLS), jnp.float32) ** shard_levels(arg_keys[2], (N_DP * OLD_CAP, COLS), ((0, 64), (1, 8)), -0.2, 0.2)), 0.1, 3.0),
        "old_offsets": draw_old_offsets(jax.random.fold_in(arg_keys[6], 71), 0),
        "activations": centred(arg_keys[4], (TOKENS, D), 1.0, 6.0, ((0, 512),)),
        "upstream": centred(arg_keys[5], (TOKENS, COLS), (TOKENS ** -0.5), 0.0625, ((0, 64), (1, 8))),
    }


beta_one = 0.9
beta_two = 0.95
epsilon = 1e-08
learn_rate = 0.05
decay_rate = 0.2

def source_rows(old_offsets, capacity):
    position = jnp.arange(D, dtype=jnp.int32)
    interior = old_offsets[1:-1]
    holder = lax.optimization_barrier(jnp.sum((position[:, None] >= interior[None, :]).astype(jnp.int32), axis=1))
    begins = old_offsets[:-1]
    starts = lax.optimization_barrier(jnp.max(jnp.where(begins[None, :] <= position[:, None], begins[None, :], 0), axis=1))
    return (holder * capacity + position - starts).astype(jnp.int32)

def adamw_update(weight, moment_one, moment_two, gradient):
    first_new = beta_one * moment_one + (1.0 - beta_one) * gradient
    second_new = beta_two * moment_two + (1.0 - beta_two) * gradient * gradient
    first_hat = first_new / (1.0 - beta_one ** STEP)
    second_hat = second_new / (1.0 - beta_two ** STEP)
    weight_new = weight - learn_rate * (first_hat / (jnp.sqrt(second_hat) + epsilon) + decay_rate * weight)
    return (weight_new, first_new, second_new)

def reference(old_weight, old_first, old_second, old_offsets, activations, upstream):
    source = source_rows(old_offsets, OLD_CAP)
    weight = old_weight[source]
    moment_one = old_first[source]
    moment_two = old_second[source]
    weight_half = weight.astype(jnp.bfloat16)
    gradient = lax.dot_general(activations, upstream, (((0,), (0,)), ((), ())), preferred_element_type=jnp.float32)
    act_grad = lax.dot_general(upstream, weight_half, (((1,), (1,)), ((), ())), preferred_element_type=jnp.float32)
    weight_new, first_new, second_new = adamw_update(weight, moment_one, moment_two, gradient)
    return (weight_new, first_new, second_new, act_grad.astype(jnp.bfloat16))
```

```python
import jax
import jax.numpy as jnp
from jax import lax
from jax.experimental import pallas as pl
from jax.experimental.pallas import tpu as pltpu
from jax.sharding import PartitionSpec as P

D = 8192
STEP = 24
SHARDS = 24
CAP = 384
ROWS = 128
COLS = 448
GROUPS = 64
SPLITS = 8
TOKENS = 16
STRIPS = COLS // 8
LANES = 128

beta_one = 0.9
beta_two = 0.95
epsilon = 1e-08
learn_rate = 0.05
decay_rate = 0.2

f32 = jnp.float32
bf16 = jnp.bfloat16
PARAMS = pltpu.CompilerParams(vmem_limit_bytes=48 * 1024 * 1024)


def pack_kernel(weight_ref, first_ref, second_ref, act_ref, out_ref):
    turned = [r[...].T for r in (weight_ref, first_ref, second_ref)]
    for s in range(GROUPS):
        act = act_ref[:, s * LANES : (s + 1) * LANES].astype(f32)
        if s < STRIPS:
            tiles = [
                t[s * 8 : s * 8 + 8, q * LANES : (q + 1) * LANES]
                for q in range(CAP // LANES)
                for t in turned
            ]
        else:
            tiles = [jnp.zeros((72, LANES), f32)]
        out_ref[s] = jnp.concatenate([act] + tiles, axis=0).astype(bf16)


def pack(weight, first, second, act):
    return pl.pallas_call(
        pack_kernel,
        out_shape=jax.ShapeDtypeStruct((GROUPS, 88, LANES), bf16),
        compiler_params=PARAMS,
        name="pack",
    )(weight, first, second, act)


def place_kernel(offsets_ref, slots_ref, out_ref, rows_ref):
    lane = lax.broadcasted_iota(jnp.int32, (3, 24, LANES), 2)
    for k in range(SHARDS):
        begin = offsets_ref[k]
        block = begin // LANES
        shift = begin % LANES
        slots = slots_ref[k].astype(f32)[16:]
        turned = pltpu.roll(slots, shift, 1).reshape(3, 24, LANES)
        here = pl.ds(block, 3)
        rows_ref[here] = jnp.where(lane >= shift, turned, rows_ref[here])
        after = pl.ds(block + 1, 3)
        rows_ref[after] = jnp.where(lane < shift, turned, rows_ref[after])
    out_ref[...] = rows_ref[:GROUPS].astype(bf16)


def place(offsets, slots):
    return pl.pallas_call(
        place_kernel,
        grid=(1,),
        in_specs=[
            pl.BlockSpec(memory_space=pltpu.SMEM),
            pl.BlockSpec((SHARDS, 88, LANES), lambda i: (0, 0, 0)),
        ],
        out_specs=pl.BlockSpec((GROUPS, 24, LANES), lambda i: (0, 0, 0)),
        out_shape=jax.ShapeDtypeStruct((GROUPS, 24, LANES), bf16),
        scratch_shapes=[pltpu.VMEM((GROUPS + 4, 24, LANES), f32)],
        compiler_params=PARAMS,
        name="place",
    )(offsets, slots)


def sums_kernel(state_ref, up_ref, out_ref, weight_ref):
    @pl.when(pl.program_id(0) == 0)
    def _():
        state = state_ref[:STRIPS].astype(f32)
        weight_ref[...] = state[:, :8].reshape(COLS, ROWS).T.astype(bf16)

    up = jnp.concatenate([up_ref[j] for j in range(8)], axis=1)
    sums = jnp.dot(weight_ref[...], up, preferred_element_type=f32).astype(bf16)
    for j in range(8):
        out_ref[j] = sums[:, j * LANES : (j + 1) * LANES]


def act_sums(state, up):
    return pl.pallas_call(
        sums_kernel,
        grid=(GROUPS // 8,),
        in_specs=[
            pl.BlockSpec((GROUPS, 24, LANES), lambda i: (0, 0, 0)),
            pl.BlockSpec((8, COLS, LANES), lambda i: (i, 0, 0)),
        ],
        out_specs=pl.BlockSpec((8, ROWS, LANES), lambda i: (i, 0, 0)),
        out_shape=jax.ShapeDtypeStruct((GROUPS, ROWS, LANES), bf16),
        scratch_shapes=[pltpu.VMEM((ROWS, COLS), bf16)],
        compiler_params=PARAMS,
        name="act_sums",
    )(state, up)


def total_kernel(parts_ref, out_ref):
    total = parts_ref[0, 0].astype(f32)
    for m in range(1, SPLITS):
        total = total + parts_ref[m, 0].astype(f32)
    out_ref[...] = total.T.astype(bf16)


def act_total(parts):
    return pl.pallas_call(
        total_kernel,
        grid=(8,),
        in_specs=[pl.BlockSpec((SPLITS, 1, ROWS, LANES), lambda i: (0, i, 0, 0))],
        out_specs=pl.BlockSpec((LANES, ROWS), lambda i: (i, 0)),
        out_shape=jax.ShapeDtypeStruct((8 * LANES, ROWS), bf16),
        compiler_params=PARAMS,
        name="act_total",
    )(parts)


def adamw_update(weight, moment_one, moment_two, gradient):
    first_new = beta_one * moment_one + (1.0 - beta_one) * gradient
    second_new = beta_two * moment_two + (1.0 - beta_two) * gradient * gradient
    first_hat = first_new / (1.0 - beta_one**STEP)
    second_hat = second_new / (1.0 - beta_two**STEP)
    weight_new = weight - learn_rate * (
        first_hat / (jnp.sqrt(second_hat) + epsilon) + decay_rate * weight
    )
    return (weight_new, first_new, second_new)


def update_kernel(state_ref, up_ref, act_ref, weight_ref, first_ref, second_ref, grad_ref):
    step = pl.program_id(0)
    up = jnp.concatenate([up_ref[j] for j in range(8)], axis=1)
    act = jnp.concatenate([act_ref[m, j] for j in range(8) for m in range(SPLITS)], axis=0)
    part = jnp.dot(up, act, preferred_element_type=f32)

    @pl.when(step == 0)
    def _():
        grad_ref[...] = part

    @pl.when(step > 0)
    def _():
        grad_ref[...] += part

    @pl.when(step == GROUPS // 8 - 1)
    def _():
        state = state_ref[:STRIPS].astype(f32)
        old = [state[:, a * 8 : a * 8 + 8].reshape(COLS, ROWS) for a in range(3)]
        new = adamw_update(old[0], old[1], old[2], grad_ref[...])
        for ref, value in zip((weight_ref, first_ref, second_ref), new):
            ref[...] = value.T


def update(state, up, act):
    out = jax.ShapeDtypeStruct((ROWS, COLS), f32)
    spec = pl.BlockSpec((ROWS, COLS), lambda i: (0, 0))
    return pl.pallas_call(
        update_kernel,
        grid=(GROUPS // 8,),
        in_specs=[
            pl.BlockSpec((GROUPS, 24, LANES), lambda i: (0, 0, 0)),
            pl.BlockSpec((8, COLS, LANES), lambda i: (i, 0, 0)),
            pl.BlockSpec((SPLITS, 8, TOKENS, LANES), lambda i: (0, i, 0, 0)),
        ],
        out_specs=[spec, spec, spec],
        out_shape=[out, out, out],
        scratch_shapes=[pltpu.VMEM((COLS, ROWS), f32)],
        compiler_params=PARAMS,
        name="update",
    )(state, up, act)


def exchange(x, axis):
    return lax.all_to_all(x, axis, split_axis=0, concat_axis=0, tiled=True)


def shards(old_weight, old_first, old_second, old_offsets, activations, upstream):
    up = lax.all_gather(upstream.T, "dp", axis=0)
    got = exchange(pack(old_weight, old_first, old_second, activations), "dp")
    act = lax.all_gather(got[:, :TOKENS], "mp", axis=0)
    state = exchange(place(old_offsets, got), "dp")
    sums = act_sums(state, up).reshape(SPLITS, 8, ROWS, LANES)
    act_grad = act_total(exchange(sums, "mp"))
    weight, first, second = update(state, up, act)
    return (weight, first, second, act_grad)


def solution(mesh):
    return jax.shard_map(
        shards,
        mesh=mesh,
        in_specs=(
            P("dp", "mp"),
            P("dp", "mp"),
            P("dp", "mp"),
            P(),
            P(("dp", "mp"), None),
            P("dp", "mp"),
        ),
        out_specs=(P("dp", "mp"), P("dp", "mp"), P("dp", "mp"), P("mp", "dp")),
        check_vma=False,
    )
```

```python
import jax
import jax.numpy as jnp
from jax import lax
from jax.experimental import pallas as pl
from jax.experimental.pallas import tpu as pltpu
from jax.sharding import PartitionSpec as P

D = 8192
STEP = 24
SHARDS = 24
CAP = 384
ROWS = 128
COLS = 448
GROUPS = 64
SPLITS = 8
TOKENS = 16
STRIPS = COLS // 8
LANES = 128

beta_one = 0.9
beta_two = 0.95
epsilon = 1e-08
learn_rate = 0.05
decay_rate = 0.2

f32 = jnp.float32
bf16 = jnp.bfloat16
PARAMS = pltpu.CompilerParams(vmem_limit_bytes=48 * 1024 * 1024)


def pack_kernel(weight_ref, first_ref, second_ref, act_ref, out_ref):
    turned = [r[...] for r in (weight_ref, first_ref, second_ref)]
    for s in range(GROUPS):
        act = act_ref[:, s * LANES : (s + 1) * LANES].astype(f32)
        if s < STRIPS:
            tiles = [
                t[s * 8 : s * 8 + 8, q * LANES : (q + 1) * LANES]
                for q in range(CAP // LANES)
                for t in turned
            ]
        else:
            tiles = [jnp.zeros((72, LANES), f32)]
        out_ref[s] = jnp.concatenate([act] + tiles, axis=0).astype(bf16)


def pack(weight, first, second, act):
    return pl.pallas_call(
        pack_kernel,
        out_shape=jax.ShapeDtypeStruct((GROUPS, 88, LANES), bf16),
        compiler_params=PARAMS,
        name="pack",
    )(weight, first, second, act)


def place_kernel(offsets_ref, slots_ref, out_ref, rows_ref):
    lane = lax.broadcasted_iota(jnp.int32, (3, 24, LANES), 2)
    for k in range(SHARDS):
        begin = offsets_ref[k]
        block = begin // LANES
        shift = begin % LANES
        slots = slots_ref[k].astype(f32)[16:]
        turned = pltpu.roll(slots, shift, 1).reshape(3, 24, LANES)
        here = pl.ds(block, 3)
        rows_ref[here] = jnp.where(lane >= shift, turned, rows_ref[here])
        after = pl.ds(block + 1, 3)
        rows_ref[after] = jnp.where(lane < shift, turned, rows_ref[after])
    out_ref[...] = rows_ref[:GROUPS].astype(bf16)


def place(offsets, slots):
    return pl.pallas_call(
        place_kernel,
        grid=(1,),
        in_specs=[
            pl.BlockSpec(memory_space=pltpu.SMEM),
            pl.BlockSpec((SHARDS, 88, LANES), lambda i: (0, 0, 0)),
        ],
        out_specs=pl.BlockSpec((GROUPS, 24, LANES), lambda i: (0, 0, 0)),
        out_shape=jax.ShapeDtypeStruct((GROUPS, 24, LANES), bf16),
        scratch_shapes=[pltpu.VMEM((GROUPS + 4, 24, LANES), f32)],
        compiler_params=PARAMS,
        name="place",
    )(offsets, slots)


def sums_kernel(state_ref, up_ref, out_ref, weight_ref):
    @pl.when(pl.program_id(0) == 0)
    def _():
        state = state_ref[:STRIPS].astype(f32)
        weight_ref[...] = state[:, :8].reshape(COLS, ROWS).T.astype(bf16)

    up = jnp.concatenate([up_ref[j] for j in range(8)], axis=1)
    sums = jnp.dot(weight_ref[...], up, preferred_element_type=f32).astype(bf16)
    for j in range(8):
        out_ref[j] = sums[:, j * LANES : (j + 1) * LANES]


def act_sums(state, up):
    return pl.pallas_call(
        sums_kernel,
        grid=(GROUPS // 8,),
        in_specs=[
            pl.BlockSpec((GROUPS, 24, LANES), lambda i: (0, 0, 0)),
            pl.BlockSpec((8, COLS, LANES), lambda i: (i, 0, 0)),
        ],
        out_specs=pl.BlockSpec((8, ROWS, LANES), lambda i: (i, 0, 0)),
        out_shape=jax.ShapeDtypeStruct((GROUPS, ROWS, LANES), bf16),
        scratch_shapes=[pltpu.VMEM((ROWS, COLS), bf16)],
        compiler_params=PARAMS,
        name="act_sums",
    )(state, up)


def total_kernel(parts_ref, out_ref):
    total = parts_ref[0, 0].astype(f32)
    for m in range(1, SPLITS):
        total = total + parts_ref[m, 0].astype(f32)
    out_ref[...] = total.T.astype(bf16)


def act_total(parts):
    return pl.pallas_call(
        total_kernel,
        grid=(8,),
        in_specs=[pl.BlockSpec((SPLITS, 1, ROWS, LANES), lambda i: (0, i, 0, 0))],
        out_specs=pl.BlockSpec((LANES, ROWS), lambda i: (i, 0)),
        out_shape=jax.ShapeDtypeStruct((8 * LANES, ROWS), bf16),
        compiler_params=PARAMS,
        name="act_total",
    )(parts)


def adamw_update(weight, moment_one, moment_two, gradient):
    first_new = beta_one * moment_one + (1.0 - beta_one) * gradient
    second_new = beta_two * moment_two + (1.0 - beta_two) * gradient * gradient
    first_hat = first_new / (1.0 - beta_one**STEP)
    second_hat = second_new / (1.0 - beta_two**STEP)
    weight_new = weight - learn_rate * (
        first_hat / (jnp.sqrt(second_hat) + epsilon) + decay_rate * weight
    )
    return (weight_new, first_new, second_new)


def update_kernel(state_ref, up_ref, act_ref, weight_ref, first_ref, second_ref, grad_ref):
    step = pl.program_id(0)
    up = jnp.concatenate([up_ref[j] for j in range(8)], axis=1)
    act = jnp.concatenate([act_ref[m, j] for j in range(8) for m in range(SPLITS)], axis=0)
    part = jnp.dot(up, act, preferred_element_type=f32)

    @pl.when(step == 0)
    def _():
        grad_ref[...] = part

    @pl.when(step > 0)
    def _():
        grad_ref[...] += part

    @pl.when(step == GROUPS // 8 - 1)
    def _():
        state = state_ref[:STRIPS].astype(f32)
        old = [state[:, a * 8 : a * 8 + 8].reshape(COLS, ROWS) for a in range(3)]
        new = adamw_update(old[0], old[1], old[2], grad_ref[...])
        for ref, value in zip((weight_ref, first_ref, second_ref), new):
            ref[...] = value


def update(state, up, act):
    out = jax.ShapeDtypeStruct((COLS, ROWS), f32)
    spec = pl.BlockSpec((COLS, ROWS), lambda i: (0, 0))
    return pl.pallas_call(
        update_kernel,
        grid=(GROUPS // 8,),
        in_specs=[
            pl.BlockSpec((GROUPS, 24, LANES), lambda i: (0, 0, 0)),
            pl.BlockSpec((8, COLS, LANES), lambda i: (i, 0, 0)),
            pl.BlockSpec((SPLITS, 8, TOKENS, LANES), lambda i: (0, i, 0, 0)),
        ],
        out_specs=[spec, spec, spec],
        out_shape=[out, out, out],
        scratch_shapes=[pltpu.VMEM((COLS, ROWS), f32)],
        compiler_params=PARAMS,
        name="update",
    )(state, up, act)


def exchange(x, axis):
    return lax.all_to_all(x, axis, split_axis=0, concat_axis=0, tiled=True)


def shards(old_weight, old_first, old_second, old_offsets, activations, upstream):
    up = lax.all_gather(upstream.T, "dp", axis=0)
    got = exchange(pack(old_weight.T, old_first.T, old_second.T, activations), "dp")
    copies = jnp.broadcast_to(got[None, :, :TOKENS], (SPLITS, GROUPS, TOKENS, LANES))
    act = exchange(copies, "mp")
    state = exchange(place(old_offsets, got), "dp")
    sums = act_sums(state, up).reshape(SPLITS, 8, ROWS, LANES)
    act_grad = act_total(exchange(sums, "mp"))
    weight, first, second = update(state, up, act)
    return (weight.T, first.T, second.T, act_grad)


def solution(mesh):
    return jax.shard_map(
        shards,
        mesh=mesh,
        in_specs=(
            P("dp", "mp"),
            P("dp", "mp"),
            P("dp", "mp"),
            P(),
            P(("dp", "mp"), None),
            P("dp", "mp"),
        ),
        out_specs=(P("dp", "mp"), P("dp", "mp"), P("dp", "mp"), P("mp", "dp")),
        check_vma=False,
    )
```

```python
import jax
import jax.numpy as jnp
from jax import lax
from jax.experimental import pallas as pl
from jax.experimental.pallas import tpu as pltpu
from jax.sharding import Mesh
from jax.sharding import PartitionSpec as P

D = 8192
STEP = 24
SHARDS = 24
CAP = 384
ROWS = 128
COLS = 448
GROUPS = 64
SPLITS = 8
TOKENS = 16
SIDE = 8
STRIPS = COLS // 8
LANES = 128

beta_one = 0.9
beta_two = 0.95
epsilon = 1e-08
learn_rate = 0.05
decay_rate = 0.2

f32 = jnp.float32
bf16 = jnp.bfloat16
PARAMS = pltpu.CompilerParams(vmem_limit_bytes=48 * 1024 * 1024)


def pack_kernel(weight_ref, first_ref, second_ref, out_ref):
    for s in range(STRIPS):
        tiles = [
            r[s * 8 : s * 8 + 8, q * LANES : (q + 1) * LANES]
            for q in range(CAP // LANES)
            for r in (weight_ref, first_ref, second_ref)
        ]
        out_ref[s] = jnp.concatenate(tiles, axis=0).astype(bf16)
    out_ref[STRIPS:] = jnp.zeros((GROUPS - STRIPS, 72, LANES), bf16)


def pack(weight, first, second):
    return pl.pallas_call(
        pack_kernel,
        out_shape=jax.ShapeDtypeStruct((GROUPS, 72, LANES), bf16),
        compiler_params=PARAMS,
        name="pack",
    )(weight, first, second)


def place_kernel(offsets_ref, slots_ref, out_ref, rows_ref):
    lane = lax.broadcasted_iota(jnp.int32, (3, 24, LANES), 2)
    for k in range(SHARDS):
        begin = offsets_ref[k]
        block = begin // LANES
        shift = begin % LANES
        slots = slots_ref[k].astype(f32)
        turned = pltpu.roll(slots, shift, 1).reshape(3, 24, LANES)
        here = pl.ds(block, 3)
        rows_ref[here] = jnp.where(lane >= shift, turned, rows_ref[here])
        after = pl.ds(block + 1, 3)
        rows_ref[after] = jnp.where(lane < shift, turned, rows_ref[after])
    for z in range(SIDE):
        rows = rows_ref[z * SIDE : (z + 1) * SIDE]
        weights = rows[:, :8].reshape(64, LANES)
        for y in range(SIDE):
            both = jnp.concatenate([weights, rows[y, 8:]], axis=0)
            out_ref[z * SIDE + y] = both.astype(bf16)


def place(offsets, slots):
    return pl.pallas_call(
        place_kernel,
        grid=(1,),
        in_specs=[
            pl.BlockSpec(memory_space=pltpu.SMEM),
            pl.BlockSpec((SHARDS, 72, LANES), lambda i: (0, 0, 0)),
        ],
        out_specs=pl.BlockSpec((GROUPS, 80, LANES), lambda i: (0, 0, 0)),
        out_shape=jax.ShapeDtypeStruct((GROUPS, 80, LANES), bf16),
        scratch_shapes=[pltpu.VMEM((GROUPS + 4, 24, LANES), f32)],
        compiler_params=PARAMS,
        name="place",
    )(offsets, slots)


def own_core(up_ref, core):
    parts = [jnp.where(core == 0, up_ref[z, 0], up_ref[z, 1]) for z in range(SIDE)]
    return jnp.concatenate(parts, axis=1)


def sums_kernel(place_ref, state_ref, up_ref, out_ref):
    up = own_core(up_ref, place_ref[1])
    state = state_ref[:STRIPS].astype(f32)
    for y in range(SIDE):
        weight = state[:, y * 8 : y * 8 + 8].reshape(COLS, ROWS).T.astype(bf16)
        sums = jnp.dot(weight, up, preferred_element_type=f32).astype(bf16)
        for z in range(SIDE):
            out_ref[z, y] = sums[:, z * LANES : (z + 1) * LANES]


def act_sums(place, state, up):
    return pl.pallas_call(
        sums_kernel,
        in_specs=[
            pl.BlockSpec(memory_space=pltpu.SMEM),
            pl.BlockSpec(memory_space=pltpu.VMEM),
            pl.BlockSpec(memory_space=pltpu.VMEM),
        ],
        out_shape=jax.ShapeDtypeStruct((SIDE, SIDE, ROWS, LANES), bf16),
        compiler_params=PARAMS,
        name="act_sums",
    )(place, state, up)


def total_kernel(parts_ref, out_ref):
    total = parts_ref[0, 0].astype(f32)
    for m in range(1, SPLITS):
        total = total + parts_ref[m, 0].astype(f32)
    out_ref[0] = total.T.astype(bf16)


def act_total(parts):
    return pl.pallas_call(
        total_kernel,
        grid=(SIDE,),
        in_specs=[pl.BlockSpec((SPLITS, 1, ROWS, LANES), lambda i: (0, i, 0, 0))],
        out_specs=pl.BlockSpec((1, LANES, ROWS), lambda i: (i, 0, 0)),
        out_shape=jax.ShapeDtypeStruct((SIDE, LANES, ROWS), bf16),
        compiler_params=PARAMS,
        name="act_total",
    )(parts)


def grad_kernel(place_ref, up_ref, act_ref, out_ref):
    up = own_core(up_ref, place_ref[1])
    act = jnp.concatenate(
        [act_ref[m, z, 0] for z in range(SIDE) for m in range(SPLITS)], axis=0
    )
    out_ref[0] = jnp.dot(up, act, preferred_element_type=f32)


def grad_parts(place, up, act):
    return pl.pallas_call(
        grad_kernel,
        grid=(SIDE,),
        in_specs=[
            pl.BlockSpec(memory_space=pltpu.SMEM),
            pl.BlockSpec((SIDE, 2, COLS, LANES), lambda i: (0, 0, 0, 0)),
            pl.BlockSpec((SPLITS, SIDE, 1, TOKENS, LANES), lambda i: (0, 0, i, 0, 0)),
        ],
        out_specs=pl.BlockSpec((1, COLS, ROWS), lambda i: (i, 0, 0)),
        out_shape=jax.ShapeDtypeStruct((SIDE, COLS, ROWS), f32),
        compiler_params=PARAMS,
        name="grad_parts",
    )(place, up, act)


def adamw_update(weight, moment_one, moment_two, gradient):
    first_new = beta_one * moment_one + (1.0 - beta_one) * gradient
    second_new = beta_two * moment_two + (1.0 - beta_two) * gradient * gradient
    first_hat = first_new / (1.0 - beta_one**STEP)
    second_hat = second_new / (1.0 - beta_two**STEP)
    weight_new = weight - learn_rate * (
        first_hat / (jnp.sqrt(second_hat) + epsilon) + decay_rate * weight
    )
    return (weight_new, first_new, second_new)


def update_kernel(place_ref, state_ref, grad_ref, weight_ref, first_ref, second_ref):
    mine = place_ref[0]
    state = state_ref[:STRIPS].astype(f32)
    weight = state[:, :8]
    for y in range(1, SIDE):
        weight = jnp.where(mine == y, state[:, y * 8 : y * 8 + 8], weight)
    old = [t.reshape(COLS, ROWS) for t in (weight, state[:, 64:72], state[:, 72:])]
    new = adamw_update(old[0], old[1], old[2], grad_ref[...])
    for ref, value in zip((weight_ref, first_ref, second_ref), new):
        ref[...] = value


def update(place, state, grad):
    out = jax.ShapeDtypeStruct((COLS, ROWS), f32)
    return pl.pallas_call(
        update_kernel,
        in_specs=[
            pl.BlockSpec(memory_space=pltpu.SMEM),
            pl.BlockSpec(memory_space=pltpu.VMEM),
            pl.BlockSpec(memory_space=pltpu.VMEM),
        ],
        out_shape=[out, out, out],
        compiler_params=PARAMS,
        name="update",
    )(place, state, grad)


def exchange(x, axis):
    return lax.all_to_all(x, axis, split_axis=0, concat_axis=0, tiled=True)


def shards(old_weight, old_first, old_second, old_offsets, activations, upstream):
    here = jnp.stack([lax.axis_index("y"), lax.axis_index("c")])
    up = lax.all_gather(upstream.T, ("z", "c"), axis=0).reshape(SIDE, 2, COLS, LANES)
    blocks = activations.reshape(TOKENS, SIDE, SIDE, LANES).transpose(1, 2, 0, 3)
    mine = exchange(blocks, "z")
    act = lax.all_gather(mine, ("x", "c"), axis=0)
    got = exchange(pack(old_weight.T, old_first.T, old_second.T), ("z", "y"))
    state = exchange(place(old_offsets, got), ("z", "y"))
    sums = act_sums(here, state, up)
    total = act_total(exchange(sums, ("x", "c")))
    act_grad = exchange(total, "y").reshape(SIDE * LANES, ROWS)
    parts = grad_parts(here, up, act)
    grad = lax.psum_scatter(parts, "y", scatter_dimension=0)
    weight, first, second = update(here, state, grad)
    return (weight.T, first.T, second.T, act_grad)


def solution(mesh):
    grid = Mesh(mesh.devices.reshape(SIDE, SIDE, SPLITS // 2, 2), ("z", "y", "x", "c"))
    dp, mp = ("z", "y"), ("x", "c")
    return jax.shard_map(
        shards,
        mesh=grid,
        in_specs=(P(dp, mp), P(dp, mp), P(dp, mp), P(), P(dp + mp, None), P(dp, mp)),
        out_specs=(P(dp, mp), P(dp, mp), P(dp, mp), P(mp, dp)),
        check_vma=False,
    )
```

```python
import jax
import jax.numpy as jnp
from jax import lax
from jax.experimental import pallas as pl
from jax.experimental.pallas import tpu as pltpu
from jax.sharding import Mesh
from jax.sharding import PartitionSpec as P

D = 8192
STEP = 24
SHARDS = 24
CAP = 384
ROWS = 128
COLS = 448
GROUPS = 64
SPLITS = 8
TOKENS = 16
SIDE = 8
STRIPS = COLS // 8
LANES = 128

beta_one = 0.9
beta_two = 0.95
epsilon = 1e-08
learn_rate = 0.05
decay_rate = 0.2

f32 = jnp.float32
bf16 = jnp.bfloat16
PARAMS = pltpu.CompilerParams(vmem_limit_bytes=48 * 1024 * 1024)


def pack_kernel(weight_ref, first_ref, second_ref, out_ref):
    for s in range(STRIPS):
        tiles = [
            r[s * 8 : s * 8 + 8, q * LANES : (q + 1) * LANES]
            for q in range(CAP // LANES)
            for r in (weight_ref, first_ref, second_ref)
        ]
        out_ref[s] = jnp.concatenate(tiles, axis=0).astype(bf16)
    out_ref[STRIPS:] = jnp.zeros((GROUPS - STRIPS, 72, LANES), bf16)


def pack(weight, first, second):
    return pl.pallas_call(
        pack_kernel,
        out_shape=jax.ShapeDtypeStruct((GROUPS, 72, LANES), bf16),
        compiler_params=PARAMS,
        name="pack",
    )(weight, first, second)


def place_kernel(offsets_ref, slots_ref, out_ref, rows_ref):
    lane = lax.broadcasted_iota(jnp.int32, (3, 24, LANES), 2)
    for k in range(SHARDS):
        begin = offsets_ref[k]
        block = begin // LANES
        shift = begin % LANES
        slots = slots_ref[k].astype(f32)
        turned = pltpu.roll(slots, shift, 1).reshape(3, 24, LANES)
        here = pl.ds(block, 3)
        rows_ref[here] = jnp.where(lane >= shift, turned, rows_ref[here])
        after = pl.ds(block + 1, 3)
        rows_ref[after] = jnp.where(lane < shift, turned, rows_ref[after])
    for z in range(SIDE):
        rows = rows_ref[z * SIDE : (z + 1) * SIDE]
        weights = rows[:, :8].reshape(64, LANES)
        for y in range(SIDE):
            both = jnp.concatenate([weights, rows[y, 8:]], axis=0)
            out_ref[z * SIDE + y] = both.astype(bf16)


def place(offsets, slots):
    return pl.pallas_call(
        place_kernel,
        grid=(1,),
        in_specs=[
            pl.BlockSpec(memory_space=pltpu.SMEM),
            pl.BlockSpec((SHARDS, 72, LANES), lambda i: (0, 0, 0)),
        ],
        out_specs=pl.BlockSpec((GROUPS, 80, LANES), lambda i: (0, 0, 0)),
        out_shape=jax.ShapeDtypeStruct((GROUPS, 80, LANES), bf16),
        scratch_shapes=[pltpu.VMEM((GROUPS + 4, 24, LANES), f32)],
        compiler_params=PARAMS,
        name="place",
    )(offsets, slots)


def send_kernel(place_ref, act_ref, *out_refs):
    for s, out_ref in enumerate(out_refs):
        z = lax.rem(place_ref[0] + s, SIDE)
        for y in range(SIDE):
            at = pl.multiple_of((z * SIDE + y) * LANES, LANES)
            out_ref[y * TOKENS : (y + 1) * TOKENS] = act_ref[:, pl.ds(at, LANES)]


def send_blocks(place, act):
    return pl.pallas_call(
        send_kernel,
        in_specs=[
            pl.BlockSpec(memory_space=pltpu.SMEM),
            pl.BlockSpec(memory_space=pltpu.VMEM),
        ],
        out_shape=[jax.ShapeDtypeStruct((SIDE * TOKENS, LANES), bf16)] * SIDE,
        compiler_params=PARAMS,
        name="send_blocks",
    )(place, act)


def sums_kernel(place_ref, own_ref, other_ref, up_ref, out_ref):
    core = place_ref[3]
    halves = []
    for c in (core, 1 - core):
        halves.append(jnp.concatenate([up_ref[2 * x + core, c] for x in range(4)], axis=1))
    up = jnp.concatenate(halves, axis=0)
    own = own_ref[...].astype(f32)
    other = other_ref[...].astype(f32)
    for y in range(SIDE):
        weight = jnp.concatenate(
            [w[:, y * 8 : y * 8 + 8].reshape(COLS, ROWS) for w in (own, other)], axis=0
        )
        sums = jnp.dot(weight.T.astype(bf16), up, preferred_element_type=f32).astype(bf16)
        for x in range(4):
            out_ref[x, y] = sums[:, x * LANES : (x + 1) * LANES]


def act_sums(place, own, other, up):
    vmem = pl.BlockSpec(memory_space=pltpu.VMEM)
    return pl.pallas_call(
        sums_kernel,
        in_specs=[pl.BlockSpec(memory_space=pltpu.SMEM)] + [vmem] * 3,
        out_shape=jax.ShapeDtypeStruct((SPLITS // 2, SIDE, ROWS, LANES), bf16),
        compiler_params=PARAMS,
        name="act_sums",
    )(place, own, other, up)


def total_kernel(parts_ref, out_ref):
    total = parts_ref[0, 0].astype(f32)
    for m in range(1, SPLITS // 2):
        total = total + parts_ref[m, 0].astype(f32)
    out_ref[0] = total.T.astype(bf16)


def act_total(parts):
    return pl.pallas_call(
        total_kernel,
        grid=(SIDE,),
        in_specs=[pl.BlockSpec((SPLITS // 2, 1, ROWS, LANES), lambda i: (0, i, 0, 0))],
        out_specs=pl.BlockSpec((1, LANES, ROWS), lambda i: (i, 0, 0)),
        out_shape=jax.ShapeDtypeStruct((SIDE, LANES, ROWS), bf16),
        compiler_params=PARAMS,
        name="act_total",
    )(parts)


def grad_kernel(place_ref, own_ref, other_ref, up_ref, out_ref):
    up = jnp.concatenate([up_ref[z, place_ref[3]] for z in range(SIDE)], axis=1)
    for y in range(0, SIDE, 2):
        act = []
        for rows in (slice(y * TOKENS, (y + 1) * TOKENS), slice((y + 1) * TOKENS, (y + 2) * TOKENS)):
            tiles = []
            for z in range(SIDE):
                back = lax.rem(place_ref[0] + SIDE - z, SIDE)
                for m in range(SPLITS):
                    x = lax.rem(place_ref[2] + 4 - m // 2, 4)
                    same = place_ref[3] == m % 2
                    tiles.append(jnp.where(same, own_ref[x, back, rows], other_ref[x, back, rows]))
            act.append(jnp.concatenate(tiles, axis=0))
        part = jnp.dot(up, jnp.concatenate(act, axis=1), preferred_element_type=f32)
        out_ref[y] = part[:, :LANES]
        out_ref[y + 1] = part[:, LANES:]


def grad_parts(place, own, other, up):
    vmem = pl.BlockSpec(memory_space=pltpu.VMEM)
    return pl.pallas_call(
        grad_kernel,
        in_specs=[pl.BlockSpec(memory_space=pltpu.SMEM)] + [vmem] * 3,
        out_shape=jax.ShapeDtypeStruct((SIDE, COLS, ROWS), f32),
        compiler_params=PARAMS,
        name="grad_parts",
    )(place, own, other, up)


def adamw_update(weight, moment_one, moment_two, gradient):
    first_new = beta_one * moment_one + (1.0 - beta_one) * gradient
    second_new = beta_two * moment_two + (1.0 - beta_two) * gradient * gradient
    first_hat = first_new / (1.0 - beta_one**STEP)
    second_hat = second_new / (1.0 - beta_two**STEP)
    weight_new = weight - learn_rate * (
        first_hat / (jnp.sqrt(second_hat) + epsilon) + decay_rate * weight
    )
    return (weight_new, first_new, second_new)


def update_kernel(place_ref, state_ref, grad_ref, weight_ref, first_ref, second_ref):
    mine = place_ref[1]
    state = state_ref[:STRIPS].astype(f32)
    weight = state[:, :8]
    for y in range(1, SIDE):
        weight = jnp.where(mine == y, state[:, y * 8 : y * 8 + 8], weight)
    old = [t.reshape(COLS, ROWS) for t in (weight, state[:, 64:72], state[:, 72:])]
    new = adamw_update(old[0], old[1], old[2], grad_ref[...])
    for ref, value in zip((weight_ref, first_ref, second_ref), new):
        ref[...] = value


def update(place, state, grad):
    out = jax.ShapeDtypeStruct((COLS, ROWS), f32)
    return pl.pallas_call(
        update_kernel,
        in_specs=[
            pl.BlockSpec(memory_space=pltpu.SMEM),
            pl.BlockSpec(memory_space=pltpu.VMEM),
            pl.BlockSpec(memory_space=pltpu.VMEM),
        ],
        out_shape=[out, out, out],
        compiler_params=PARAMS,
        name="update",
    )(place, state, grad)


def exchange(x, axis):
    return lax.all_to_all(x, axis, split_axis=0, concat_axis=0, tiled=True)


def shift(x, axis, by):
    n = lax.axis_size(axis)
    return lax.ppermute(x, axis, [(i, (i + by) % n) for i in range(n)])


def shards(old_weight, old_first, old_second, old_offsets, activations, upstream):
    here = jnp.stack([lax.axis_index(a) for a in ("z", "y", "x", "c")])
    up = lax.all_gather(upstream.T, ("z", "c"), axis=0).reshape(SIDE, 2, COLS, LANES)
    got = exchange(pack(old_weight.T, old_first.T, old_second.T), ("z", "y"))
    sent = send_blocks(here, activations)
    act = jnp.stack([sent[0]] + [shift(sent[s], "z", s) for s in range(1, SIDE)])
    got, act = lax.optimization_barrier((got, act))
    own = jnp.stack([act] + [shift(act, "x", s) for s in range(1, SPLITS // 2)])
    state = exchange(place(old_offsets, got), ("z", "y"))
    parts = grad_parts(here, own, shift(own, "c", 1), up)
    state, parts = lax.optimization_barrier((state, parts))
    grad = lax.psum_scatter(parts, "y", scatter_dimension=0)
    weight = state[:STRIPS, : SIDE * 8]
    sums = act_sums(here, weight, shift(weight, "c", 1), up)
    total = act_total(exchange(sums, "x"))
    act_grad = exchange(total, "y").reshape(SIDE * LANES, ROWS)
    weight, first, second = update(here, state, grad)
    return (weight.T, first.T, second.T, act_grad)


def solution(mesh):
    grid = Mesh(mesh.devices.reshape(SIDE, SIDE, SPLITS // 2, 2), ("z", "y", "x", "c"))
    dp, mp = ("z", "y"), ("x", "c")
    return jax.shard_map(
        shards,
        mesh=grid,
        in_specs=(P(dp, mp), P(dp, mp), P(dp, mp), P(), P(dp + mp, None), P(dp, mp)),
        out_specs=(P(dp, mp), P(dp, mp), P(dp, mp), P(mp, dp)),
        check_vma=False,
    )
```

```python
import jax
import jax.numpy as jnp
from jax import lax
from jax.experimental import pallas as pl
from jax.experimental.pallas import tpu as pltpu
from jax.sharding import Mesh
from jax.sharding import PartitionSpec as P

D = 8192
STEP = 24
SHARDS = 24
CAP = 384
ROWS = 128
COLS = 448
GROUPS = 64
SPLITS = 8
TOKENS = 16
SIDE = 8
STRIPS = COLS // 8
LANES = 128

beta_one = 0.9
beta_two = 0.95
epsilon = 1e-08
learn_rate = 0.05
decay_rate = 0.2

f32 = jnp.float32
bf16 = jnp.bfloat16
PARAMS = pltpu.CompilerParams(vmem_limit_bytes=48 * 1024 * 1024)


def pack_kernel(weight_ref, first_ref, second_ref, out_ref):
    for s in range(STRIPS):
        tiles = [
            r[s * 8 : s * 8 + 8, q * LANES : (q + 1) * LANES]
            for q in range(CAP // LANES)
            for r in (weight_ref, first_ref, second_ref)
        ]
        out_ref[s] = jnp.concatenate(tiles, axis=0).astype(bf16)
    out_ref[STRIPS:] = jnp.zeros((GROUPS - STRIPS, 72, LANES), bf16)


def pack(weight, first, second):
    return pl.pallas_call(
        pack_kernel,
        out_shape=jax.ShapeDtypeStruct((GROUPS, 72, LANES), bf16),
        compiler_params=PARAMS,
        name="pack",
    )(weight, first, second)


def place_kernel(offsets_ref, slots_ref, out_ref, rows_ref):
    lane = lax.broadcasted_iota(jnp.int32, (3, 24, LANES), 2)
    for k in range(SHARDS):
        begin = offsets_ref[k]
        block = begin // LANES
        shift = begin % LANES
        slots = slots_ref[k].astype(f32)
        turned = pltpu.roll(slots, shift, 1).reshape(3, 24, LANES)
        here = pl.ds(block, 3)
        rows_ref[here] = jnp.where(lane >= shift, turned, rows_ref[here])
        after = pl.ds(block + 1, 3)
        rows_ref[after] = jnp.where(lane < shift, turned, rows_ref[after])
    for z in range(SIDE):
        rows = rows_ref[z * SIDE : (z + 1) * SIDE]
        weights = rows[:, :8].reshape(64, LANES).astype(bf16)
        for y in range(SIDE):
            out_ref[z * SIDE + y, :64] = weights
            out_ref[z * SIDE + y, 64:] = rows[y, 8:].astype(bf16)


def place(offsets, slots):
    return pl.pallas_call(
        place_kernel,
        grid=(1,),
        in_specs=[
            pl.BlockSpec(memory_space=pltpu.SMEM),
            pl.BlockSpec((SHARDS, 72, LANES), lambda i: (0, 0, 0)),
        ],
        out_specs=pl.BlockSpec((GROUPS, 80, LANES), lambda i: (0, 0, 0)),
        out_shape=jax.ShapeDtypeStruct((GROUPS, 80, LANES), bf16),
        scratch_shapes=[pltpu.VMEM((GROUPS + 4, 24, LANES), f32)],
        compiler_params=PARAMS,
        name="place",
    )(offsets, slots)


def send_kernel(place_ref, act_ref, *out_refs):
    for s, out_ref in enumerate(out_refs):
        z = lax.rem(place_ref[0] + s, SIDE)
        for y in range(SIDE):
            at = pl.multiple_of((z * SIDE + y) * LANES, LANES)
            out_ref[y * TOKENS : (y + 1) * TOKENS] = act_ref[:, pl.ds(at, LANES)]


def send_blocks(place, act):
    return pl.pallas_call(
        send_kernel,
        in_specs=[
            pl.BlockSpec(memory_space=pltpu.SMEM),
            pl.BlockSpec(memory_space=pltpu.VMEM),
        ],
        out_shape=[jax.ShapeDtypeStruct((SIDE * TOKENS, LANES), bf16)] * SIDE,
        compiler_params=PARAMS,
        name="send_blocks",
    )(place, act)


def sums_kernel(place_ref, own_ref, other_ref, up_ref, out_ref):
    core = place_ref[3]
    halves = []
    for c in (core, 1 - core):
        halves.append(jnp.concatenate([up_ref[2 * x + core, c] for x in range(4)], axis=1))
    up = jnp.concatenate(halves, axis=0)
    own = own_ref[...].astype(f32)
    other = other_ref[...].astype(f32)
    for y in range(SIDE):
        weight = jnp.concatenate(
            [w[:, y * 8 : y * 8 + 8].reshape(COLS, ROWS) for w in (own, other)], axis=0
        )
        sums = jnp.dot(weight.T.astype(bf16), up, preferred_element_type=f32).astype(bf16)
        for x in range(4):
            out_ref[x, y] = sums[:, x * LANES : (x + 1) * LANES]


def act_sums(place, own, other, up):
    vmem = pl.BlockSpec(memory_space=pltpu.VMEM)
    return pl.pallas_call(
        sums_kernel,
        in_specs=[pl.BlockSpec(memory_space=pltpu.SMEM)] + [vmem] * 3,
        out_shape=jax.ShapeDtypeStruct((SPLITS // 2, SIDE, ROWS, LANES), bf16),
        compiler_params=PARAMS,
        name="act_sums",
    )(place, own, other, up)


def total_kernel(parts_ref, out_ref):
    for y in range(SIDE):
        total = parts_ref[0, y].astype(f32)
        for x in range(1, SPLITS // 2):
            total = total + parts_ref[x, y].astype(f32)
        out_ref[y] = total.T.astype(bf16)


def act_total(parts):
    return pl.pallas_call(
        total_kernel,
        out_shape=jax.ShapeDtypeStruct((SIDE, LANES, ROWS), bf16),
        compiler_params=PARAMS,
        name="act_total",
    )(parts)


def grad_kernel(place_ref, own_ref, other_ref, up_ref, out_ref):
    up = jnp.concatenate([up_ref[z, place_ref[3]] for z in range(SIDE)], axis=1)
    for y in range(0, SIDE, 2):
        act = []
        for rows in (slice(y * TOKENS, (y + 1) * TOKENS), slice((y + 1) * TOKENS, (y + 2) * TOKENS)):
            tiles = []
            for z in range(SIDE):
                back = lax.rem(place_ref[0] + SIDE - z, SIDE)
                for m in range(SPLITS):
                    x = lax.rem(place_ref[2] + 4 - m // 2, 4)
                    same = place_ref[3] == m % 2
                    tiles.append(jnp.where(same, own_ref[x, back, rows], other_ref[x, back, rows]))
            act.append(jnp.concatenate(tiles, axis=0))
        part = jnp.dot(up, jnp.concatenate(act, axis=1), preferred_element_type=f32)
        out_ref[y] = part[:, :LANES]
        out_ref[y + 1] = part[:, LANES:]


def grad_parts(place, own, other, up):
    vmem = pl.BlockSpec(memory_space=pltpu.VMEM)
    return pl.pallas_call(
        grad_kernel,
        in_specs=[pl.BlockSpec(memory_space=pltpu.SMEM)] + [vmem] * 3,
        out_shape=jax.ShapeDtypeStruct((SIDE, COLS, ROWS), f32),
        compiler_params=PARAMS,
        name="grad_parts",
    )(place, own, other, up)


def adamw_update(weight, moment_one, moment_two, gradient):
    first_new = beta_one * moment_one + (1.0 - beta_one) * gradient
    second_new = beta_two * moment_two + (1.0 - beta_two) * gradient * gradient
    first_hat = first_new / (1.0 - beta_one**STEP)
    second_hat = second_new / (1.0 - beta_two**STEP)
    weight_new = weight - learn_rate * (
        first_hat / (jnp.sqrt(second_hat) + epsilon) + decay_rate * weight
    )
    return (weight_new, first_new, second_new)


def update_kernel(place_ref, state_ref, grad_ref, weight_ref, first_ref, second_ref):
    mine = place_ref[1]
    state = state_ref[:STRIPS].astype(f32)
    weight = state[:, :8]
    for y in range(1, SIDE):
        weight = jnp.where(mine == y, state[:, y * 8 : y * 8 + 8], weight)
    old = [t.reshape(COLS, ROWS) for t in (weight, state[:, 64:72], state[:, 72:])]
    new = adamw_update(old[0], old[1], old[2], grad_ref[...])
    for ref, value in zip((weight_ref, first_ref, second_ref), new):
        ref[...] = value


def update(place, state, grad):
    out = jax.ShapeDtypeStruct((COLS, ROWS), f32)
    return pl.pallas_call(
        update_kernel,
        in_specs=[
            pl.BlockSpec(memory_space=pltpu.SMEM),
            pl.BlockSpec(memory_space=pltpu.VMEM),
            pl.BlockSpec(memory_space=pltpu.VMEM),
        ],
        out_shape=[out, out, out],
        compiler_params=PARAMS,
        name="update",
    )(place, state, grad)


def exchange(x, axis):
    return lax.all_to_all(x, axis, split_axis=0, concat_axis=0, tiled=True)


def shift(x, axis, by):
    n = lax.axis_size(axis)
    return lax.ppermute(x, axis, [(i, (i + by) % n) for i in range(n)])


def shards(old_weight, old_first, old_second, old_offsets, activations, upstream):
    here = jnp.stack([lax.axis_index(a) for a in ("z", "y", "x", "c")])
    up = lax.all_gather(upstream.T, ("z", "c"), axis=0).reshape(SIDE, 2, COLS, LANES)
    got = exchange(pack(old_weight.T, old_first.T, old_second.T), ("z", "y"))
    sent = send_blocks(here, activations)
    act = jnp.stack([sent[0]] + [shift(sent[s], "z", s) for s in range(1, SIDE)])
    got, act = lax.optimization_barrier((got, act))
    own = jnp.stack([act] + [shift(act, "x", s) for s in range(1, SPLITS // 2)])
    own, up = lax.optimization_barrier((own, up))
    state = exchange(place(old_offsets, got), ("z", "y"))
    parts = grad_parts(here, own, shift(own, "c", 1), up)
    state, parts = lax.optimization_barrier((state, parts))
    grad = lax.psum_scatter(parts, "y", scatter_dimension=0)
    weight = state[:STRIPS, : SIDE * 8]
    sums = act_sums(here, weight, shift(weight, "c", 1), up)
    total = act_total(exchange(sums, "x"))
    last = exchange(total, "y")
    new = update(here, state, grad)
    last, (weight, first, second) = lax.optimization_barrier((last, new))
    act_grad = last.reshape(SIDE * LANES, ROWS)
    return (weight.T, first.T, second.T, act_grad)


def solution(mesh):
    grid = Mesh(mesh.devices.reshape(SIDE, SIDE, SPLITS // 2, 2), ("z", "y", "x", "c"))
    dp, mp = ("z", "y"), ("x", "c")
    return jax.shard_map(
        shards,
        mesh=grid,
        in_specs=(P(dp, mp), P(dp, mp), P(dp, mp), P(), P(dp + mp, None), P(dp, mp)),
        out_specs=(P(dp, mp), P(dp, mp), P(dp, mp), P(mp, dp)),
        check_vma=False,
    )
```

```python
import jax
import jax.numpy as jnp
from jax import lax
from jax.experimental import pallas as pl
from jax.experimental.pallas import tpu as pltpu
from jax.sharding import Mesh
from jax.sharding import PartitionSpec as P

D = 8192
STEP = 24
SHARDS = 24
CAP = 384
ROWS = 128
COLS = 448
GROUPS = 64
SPLITS = 8
TOKENS = 16
SIDE = 8
STRIPS = COLS // 8
LANES = 128

beta_one = 0.9
beta_two = 0.95
epsilon = 1e-08
learn_rate = 0.05
decay_rate = 0.2

f32 = jnp.float32
bf16 = jnp.bfloat16
PARAMS = pltpu.CompilerParams(vmem_limit_bytes=48 * 1024 * 1024)


def pack_kernel(weight_ref, first_ref, second_ref, out_ref):
    held = [r[...].astype(f32) for r in (weight_ref, first_ref, second_ref)]
    for s in range(STRIPS):
        tiles = [
            t[s * 8 : s * 8 + 8, q * LANES : (q + 1) * LANES]
            for q in range(CAP // LANES)
            for t in held
        ]
        out_ref[s] = jnp.concatenate(tiles, axis=0).astype(bf16)
    out_ref[STRIPS:] = jnp.zeros((GROUPS - STRIPS, 72, LANES), bf16)


def pack(weight, first, second):
    return pl.pallas_call(
        pack_kernel,
        out_shape=jax.ShapeDtypeStruct((GROUPS, 72, LANES), bf16),
        compiler_params=PARAMS,
        name="pack",
    )(weight, first, second)


def place_kernel(offsets_ref, slots_ref, out_ref, rows_ref):
    lane = lax.broadcasted_iota(jnp.int32, (3, 24, LANES), 2)
    for k in range(SHARDS):
        begin = offsets_ref[k]
        block = begin // LANES
        shift = begin % LANES
        slots = slots_ref[k].astype(f32)
        turned = pltpu.roll(slots, shift, 1).reshape(3, 24, LANES)
        here = pl.ds(block, 3)
        rows_ref[here] = jnp.where(lane >= shift, turned, rows_ref[here])
        after = pl.ds(block + 1, 3)
        rows_ref[after] = jnp.where(lane < shift, turned, rows_ref[after])
    for z in range(SIDE):
        rows = rows_ref[z * SIDE : (z + 1) * SIDE]
        weights = rows[:, :8].reshape(64, LANES).astype(bf16)
        for y in range(SIDE):
            out_ref[z * SIDE + y, :64] = weights
            out_ref[z * SIDE + y, 64:] = rows[y, 8:].astype(bf16)


def place(offsets, slots):
    return pl.pallas_call(
        place_kernel,
        grid=(1,),
        in_specs=[
            pl.BlockSpec(memory_space=pltpu.SMEM),
            pl.BlockSpec((SHARDS, 72, LANES), lambda i: (0, 0, 0)),
        ],
        out_specs=pl.BlockSpec((GROUPS, 80, LANES), lambda i: (0, 0, 0)),
        out_shape=jax.ShapeDtypeStruct((GROUPS, 80, LANES), bf16),
        scratch_shapes=[pltpu.VMEM((GROUPS + 4, 24, LANES), f32)],
        compiler_params=PARAMS,
        name="place",
    )(offsets, slots)


def send_kernel(place_ref, act_ref, *out_refs):
    for s, out_ref in enumerate(out_refs):
        z = lax.rem(place_ref[0] + s, SIDE)
        for y in range(SIDE):
            at = pl.multiple_of((z * SIDE + y) * LANES, LANES)
            out_ref[y * TOKENS : (y + 1) * TOKENS] = act_ref[:, pl.ds(at, LANES)]


def send_blocks(place, act):
    return pl.pallas_call(
        send_kernel,
        in_specs=[
            pl.BlockSpec(memory_space=pltpu.SMEM),
            pl.BlockSpec(memory_space=pltpu.VMEM),
        ],
        out_shape=[jax.ShapeDtypeStruct((SIDE * TOKENS, LANES), bf16)] * SIDE,
        compiler_params=PARAMS,
        name="send_blocks",
    )(place, act)


def sums_kernel(place_ref, own_ref, other_ref, up_ref, out_ref):
    core = place_ref[3]
    halves = []
    for c in (core, 1 - core):
        halves.append(jnp.concatenate([up_ref[2 * x + core, c] for x in range(4)], axis=1))
    up = jnp.concatenate(halves, axis=0)
    own = own_ref[...].astype(f32)
    other = other_ref[...].astype(f32)
    for y in range(SIDE):
        weight = jnp.concatenate(
            [w[:, y * 8 : y * 8 + 8].reshape(COLS, ROWS) for w in (own, other)], axis=0
        )
        sums = jnp.dot(weight.T.astype(bf16), up, preferred_element_type=f32).astype(bf16)
        for x in range(4):
            out_ref[x, y] = sums[:, x * LANES : (x + 1) * LANES]


def act_sums(place, own, other, up):
    vmem = pl.BlockSpec(memory_space=pltpu.VMEM)
    return pl.pallas_call(
        sums_kernel,
        in_specs=[pl.BlockSpec(memory_space=pltpu.SMEM)] + [vmem] * 3,
        out_shape=jax.ShapeDtypeStruct((SPLITS // 2, SIDE, ROWS, LANES), bf16),
        compiler_params=PARAMS,
        name="act_sums",
    )(place, own, other, up)


def total_kernel(parts_ref, out_ref):
    for y in range(SIDE):
        total = parts_ref[0, y].astype(f32)
        for x in range(1, SPLITS // 2):
            total = total + parts_ref[x, y].astype(f32)
        out_ref[y] = total.T.astype(bf16)


def act_total(parts):
    return pl.pallas_call(
        total_kernel,
        out_shape=jax.ShapeDtypeStruct((SIDE, LANES, ROWS), bf16),
        compiler_params=PARAMS,
        name="act_total",
    )(parts)


def grad_kernel(place_ref, own_ref, other_ref, up_ref, out_ref):
    up = jnp.concatenate([up_ref[z, place_ref[3]] for z in range(SIDE)], axis=1)
    for y in range(0, SIDE, 2):
        act = []
        for rows in (slice(y * TOKENS, (y + 1) * TOKENS), slice((y + 1) * TOKENS, (y + 2) * TOKENS)):
            tiles = []
            for z in range(SIDE):
                back = lax.rem(place_ref[0] + SIDE - z, SIDE)
                for m in range(SPLITS):
                    x = lax.rem(place_ref[2] + 4 - m // 2, 4)
                    same = place_ref[3] == m % 2
                    tiles.append(jnp.where(same, own_ref[x, back, rows], other_ref[x, back, rows]))
            act.append(jnp.concatenate(tiles, axis=0))
        part = jnp.dot(up, jnp.concatenate(act, axis=1), preferred_element_type=f32)
        out_ref[y] = part[:, :LANES]
        out_ref[y + 1] = part[:, LANES:]


def grad_parts(place, own, other, up):
    vmem = pl.BlockSpec(memory_space=pltpu.VMEM)
    return pl.pallas_call(
        grad_kernel,
        in_specs=[pl.BlockSpec(memory_space=pltpu.SMEM)] + [vmem] * 3,
        out_shape=jax.ShapeDtypeStruct((SIDE, COLS, ROWS), f32),
        compiler_params=PARAMS,
        name="grad_parts",
    )(place, own, other, up)


def adamw_update(weight, moment_one, moment_two, gradient):
    first_new = beta_one * moment_one + (1.0 - beta_one) * gradient
    second_new = beta_two * moment_two + (1.0 - beta_two) * gradient * gradient
    first_hat = first_new / (1.0 - beta_one**STEP)
    second_hat = second_new / (1.0 - beta_two**STEP)
    weight_new = weight - learn_rate * (
        first_hat / (jnp.sqrt(second_hat) + epsilon) + decay_rate * weight
    )
    return (weight_new, first_new, second_new)


def update_kernel(place_ref, state_ref, grad_ref, weight_ref, first_ref, second_ref):
    mine = place_ref[1]
    state = state_ref[:STRIPS].astype(f32)
    weight = state[:, :8]
    for y in range(1, SIDE):
        weight = jnp.where(mine == y, state[:, y * 8 : y * 8 + 8], weight)
    old = [t.reshape(COLS, ROWS) for t in (weight, state[:, 64:72], state[:, 72:])]
    new = adamw_update(old[0], old[1], old[2], grad_ref[...])
    for ref, value in zip((weight_ref, first_ref, second_ref), new):
        ref[...] = value


def update(place, state, grad):
    out = jax.ShapeDtypeStruct((COLS, ROWS), f32)
    return pl.pallas_call(
        update_kernel,
        in_specs=[
            pl.BlockSpec(memory_space=pltpu.SMEM),
            pl.BlockSpec(memory_space=pltpu.VMEM),
            pl.BlockSpec(memory_space=pltpu.VMEM),
        ],
        out_shape=[out, out, out],
        compiler_params=PARAMS,
        name="update",
    )(place, state, grad)


def exchange(x, axis):
    return lax.all_to_all(x, axis, split_axis=0, concat_axis=0, tiled=True)


def shift(x, axis, by):
    n = lax.axis_size(axis)
    return lax.ppermute(x, axis, [(i, (i + by) % n) for i in range(n)])


def shards(old_weight, old_first, old_second, old_offsets, activations, upstream):
    here = jnp.stack([lax.axis_index(a) for a in ("z", "y", "x", "c")])
    up = lax.all_gather(upstream.T, ("z", "c"), axis=0).reshape(SIDE, 2, COLS, LANES)
    halves = [t.T.astype(bf16) for t in (old_weight, old_first, old_second)]
    got = exchange(pack(*halves), ("z", "y"))
    sent = send_blocks(here, activations)
    act = jnp.stack([sent[0]] + [shift(sent[s], "z", s) for s in range(1, SIDE)])
    got, act = lax.optimization_barrier((got, act))
    own = jnp.stack([act] + [shift(act, "x", s) for s in range(1, SPLITS // 2)])
    own, up = lax.optimization_barrier((own, up))
    state = exchange(place(old_offsets, got), ("z", "y"))
    parts = grad_parts(here, own, shift(own, "c", 1), up)
    state, parts = lax.optimization_barrier((state, parts))
    grad = lax.psum_scatter(parts, "y", scatter_dimension=0)
    weight = state[:STRIPS, : SIDE * 8]
    sums = act_sums(here, weight, shift(weight, "c", 1), up)
    total = act_total(exchange(sums, "x"))
    last = exchange(total, "y")
    new = update(here, state, grad)
    last, (weight, first, second) = lax.optimization_barrier((last, new))
    act_grad = last.reshape(SIDE * LANES, ROWS)
    return (weight.T, first.T, second.T, act_grad)


def solution(mesh):
    grid = Mesh(mesh.devices.reshape(SIDE, SIDE, SPLITS // 2, 2), ("z", "y", "x", "c"))
    dp, mp = ("z", "y"), ("x", "c")
    return jax.shard_map(
        shards,
        mesh=grid,
        in_specs=(P(dp, mp), P(dp, mp), P(dp, mp), P(), P(dp + mp, None), P(dp, mp)),
        out_specs=(P(dp, mp), P(dp, mp), P(dp, mp), P(mp, dp)),
        check_vma=False,
    )
```

```python
import jax
import jax.numpy as jnp
from jax import lax
from jax.experimental import pallas as pl
from jax.experimental.pallas import tpu as pltpu
from jax.sharding import Mesh
from jax.sharding import PartitionSpec as P

D = 8192
STEP = 24
SHARDS = 24
CAP = 384
ROWS = 128
COLS = 448
GROUPS = 64
SPLITS = 8
TOKENS = 16
SIDE = 8
STRIPS = COLS // 8
LANES = 128

beta_one = 0.9
beta_two = 0.95
epsilon = 1e-08
learn_rate = 0.05
decay_rate = 0.2

f32 = jnp.float32
bf16 = jnp.bfloat16
PARAMS = pltpu.CompilerParams(vmem_limit_bytes=48 * 1024 * 1024)


def pack_kernel(weight_ref, first_ref, second_ref, out_ref):
    held = [r[...].astype(f32) for r in (weight_ref, first_ref, second_ref)]
    for s in range(STRIPS):
        tiles = [
            t[s * 8 : s * 8 + 8, q * LANES : (q + 1) * LANES]
            for q in range(CAP // LANES)
            for t in held
        ]
        out_ref[s] = jnp.concatenate(tiles, axis=0).astype(bf16)
    out_ref[STRIPS:] = jnp.zeros((GROUPS - STRIPS, 72, LANES), bf16)


def pack(weight, first, second):
    return pl.pallas_call(
        pack_kernel,
        out_shape=jax.ShapeDtypeStruct((GROUPS, 72, LANES), bf16),
        compiler_params=PARAMS,
        name="pack",
    )(weight, first, second)


def place_kernel(offsets_ref, slots_ref, out_ref, rows_ref):
    lane = lax.broadcasted_iota(jnp.int32, (24, LANES), 1)
    for k in range(SHARDS):
        begin = offsets_ref[k]
        block = begin // LANES
        shift = begin % LANES
        turned = pltpu.roll(slots_ref[k].astype(f32), shift, 1).reshape(3, 24, LANES)
        rows_ref[block] = jnp.where(lane >= shift, turned[0], rows_ref[block])
        rows_ref[block + 1] = jnp.where(lane >= shift, turned[1], turned[0])
        rows_ref[block + 2] = jnp.where(lane >= shift, turned[2], turned[1])
        rows_ref[block + 3] = turned[2]
    for z in range(SIDE):
        rows = rows_ref[z * SIDE : (z + 1) * SIDE]
        weights = rows[:, :8].reshape(64, LANES).astype(bf16)
        for y in range(SIDE):
            out_ref[z * SIDE + y, :64] = weights
            out_ref[z * SIDE + y, 64:] = rows[y, 8:].astype(bf16)


def place(offsets, slots):
    return pl.pallas_call(
        place_kernel,
        grid=(1,),
        in_specs=[
            pl.BlockSpec(memory_space=pltpu.SMEM),
            pl.BlockSpec((SHARDS, 72, LANES), lambda i: (0, 0, 0)),
        ],
        out_specs=pl.BlockSpec((GROUPS, 80, LANES), lambda i: (0, 0, 0)),
        out_shape=jax.ShapeDtypeStruct((GROUPS, 80, LANES), bf16),
        scratch_shapes=[pltpu.VMEM((GROUPS + 4, 24, LANES), f32)],
        compiler_params=PARAMS,
        name="place",
    )(offsets, slots)


def send_kernel(place_ref, act_ref, *out_refs):
    for s, out_ref in enumerate(out_refs):
        z = lax.rem(place_ref[0] + s, SIDE)
        for y in range(SIDE):
            at = pl.multiple_of((z * SIDE + y) * LANES, LANES)
            out_ref[y * TOKENS : (y + 1) * TOKENS] = act_ref[:, pl.ds(at, LANES)]


def send_blocks(place, act):
    return pl.pallas_call(
        send_kernel,
        in_specs=[
            pl.BlockSpec(memory_space=pltpu.SMEM),
            pl.BlockSpec(memory_space=pltpu.VMEM),
        ],
        out_shape=[jax.ShapeDtypeStruct((SIDE * TOKENS, LANES), bf16)] * SIDE,
        compiler_params=PARAMS,
        name="send_blocks",
    )(place, act)


def sums_kernel(place_ref, own_ref, other_ref, up_ref, out_ref):
    core = place_ref[3]
    halves = []
    for c in (core, 1 - core):
        halves.append(jnp.concatenate([up_ref[2 * x + core, c] for x in range(4)], axis=1))
    up = jnp.concatenate(halves, axis=0)
    own = own_ref[...].astype(f32)
    other = other_ref[...].astype(f32)
    for y in range(SIDE):
        weight = jnp.concatenate(
            [w[:, y * 8 : y * 8 + 8].reshape(COLS, ROWS) for w in (own, other)], axis=0
        )
        sums = jnp.dot(weight.T.astype(bf16), up, preferred_element_type=f32).astype(bf16)
        for x in range(4):
            out_ref[x, y] = sums[:, x * LANES : (x + 1) * LANES]


def act_sums(place, own, other, up):
    vmem = pl.BlockSpec(memory_space=pltpu.VMEM)
    return pl.pallas_call(
        sums_kernel,
        in_specs=[pl.BlockSpec(memory_space=pltpu.SMEM)] + [vmem] * 3,
        out_shape=jax.ShapeDtypeStruct((SPLITS // 2, SIDE, ROWS, LANES), bf16),
        compiler_params=PARAMS,
        name="act_sums",
    )(place, own, other, up)


def total_kernel(parts_ref, out_ref):
    for y in range(SIDE):
        total = parts_ref[0, y].astype(f32)
        for x in range(1, SPLITS // 2):
            total = total + parts_ref[x, y].astype(f32)
        out_ref[y] = total.T.astype(bf16)


def act_total(parts):
    return pl.pallas_call(
        total_kernel,
        out_shape=jax.ShapeDtypeStruct((SIDE, LANES, ROWS), bf16),
        compiler_params=PARAMS,
        name="act_total",
    )(parts)


def grad_kernel(place_ref, own_ref, other_ref, up_ref, out_ref):
    up = jnp.concatenate([up_ref[z, place_ref[3]] for z in range(SIDE)], axis=1)
    for y in range(0, SIDE, 2):
        act = []
        for rows in (slice(y * TOKENS, (y + 1) * TOKENS), slice((y + 1) * TOKENS, (y + 2) * TOKENS)):
            tiles = []
            for z in range(SIDE):
                back = lax.rem(place_ref[0] + SIDE - z, SIDE)
                for m in range(SPLITS):
                    x = lax.rem(place_ref[2] + 4 - m // 2, 4)
                    same = place_ref[3] == m % 2
                    tiles.append(jnp.where(same, own_ref[x, back, rows], other_ref[x, back, rows]))
            act.append(jnp.concatenate(tiles, axis=0))
        part = jnp.dot(up, jnp.concatenate(act, axis=1), preferred_element_type=f32)
        out_ref[y] = part[:, :LANES]
        out_ref[y + 1] = part[:, LANES:]


def grad_parts(place, own, other, up):
    vmem = pl.BlockSpec(memory_space=pltpu.VMEM)
    return pl.pallas_call(
        grad_kernel,
        in_specs=[pl.BlockSpec(memory_space=pltpu.SMEM)] + [vmem] * 3,
        out_shape=jax.ShapeDtypeStruct((SIDE, COLS, ROWS), f32),
        compiler_params=PARAMS,
        name="grad_parts",
    )(place, own, other, up)


def adamw_update(weight, moment_one, moment_two, gradient):
    first_new = beta_one * moment_one + (1.0 - beta_one) * gradient
    second_new = beta_two * moment_two + (1.0 - beta_two) * gradient * gradient
    first_hat = first_new / (1.0 - beta_one**STEP)
    second_hat = second_new / (1.0 - beta_two**STEP)
    weight_new = weight - learn_rate * (
        first_hat / (jnp.sqrt(second_hat) + epsilon) + decay_rate * weight
    )
    return (weight_new, first_new, second_new)


def update_kernel(place_ref, state_ref, grad_ref, weight_ref, first_ref, second_ref):
    mine = place_ref[1]
    state = state_ref[:STRIPS].astype(f32)
    weight = state[:, :8]
    for y in range(1, SIDE):
        weight = jnp.where(mine == y, state[:, y * 8 : y * 8 + 8], weight)
    old = [t.reshape(COLS, ROWS) for t in (weight, state[:, 64:72], state[:, 72:])]
    new = adamw_update(old[0], old[1], old[2], grad_ref[...])
    for ref, value in zip((weight_ref, first_ref, second_ref), new):
        ref[...] = value


def update(place, state, grad):
    out = jax.ShapeDtypeStruct((COLS, ROWS), f32)
    return pl.pallas_call(
        update_kernel,
        in_specs=[
            pl.BlockSpec(memory_space=pltpu.SMEM),
            pl.BlockSpec(memory_space=pltpu.VMEM),
            pl.BlockSpec(memory_space=pltpu.VMEM),
        ],
        out_shape=[out, out, out],
        compiler_params=PARAMS,
        name="update",
    )(place, state, grad)


def exchange(x, axis):
    return lax.all_to_all(x, axis, split_axis=0, concat_axis=0, tiled=True)


def shift(x, axis, by):
    n = lax.axis_size(axis)
    return lax.ppermute(x, axis, [(i, (i + by) % n) for i in range(n)])


def shards(old_weight, old_first, old_second, old_offsets, activations, upstream):
    here = jnp.stack([lax.axis_index(a) for a in ("z", "y", "x", "c")])
    up = lax.all_gather(upstream.T, ("z", "c"), axis=0).reshape(SIDE, 2, COLS, LANES)
    halves = [t.T.astype(bf16) for t in (old_weight, old_first, old_second)]
    got = exchange(pack(*halves), ("z", "y"))
    sent = send_blocks(here, activations)
    act = jnp.stack([sent[0]] + [shift(sent[s], "z", s) for s in range(1, SIDE)])
    got, act = lax.optimization_barrier((got, act))
    own = jnp.stack([act] + [shift(act, "x", s) for s in range(1, SPLITS // 2)])
    own, up = lax.optimization_barrier((own, up))
    state = exchange(place(old_offsets, got), ("z", "y"))
    parts = grad_parts(here, own, shift(own, "c", 1), up)
    state, parts = lax.optimization_barrier((state, parts))
    grad = lax.psum_scatter(parts, "y", scatter_dimension=0)
    weight = state[:STRIPS, : SIDE * 8]
    sums = act_sums(here, weight, shift(weight, "c", 1), up)
    total = act_total(exchange(sums, "x"))
    last = exchange(total, "y")
    new = update(here, state, grad)
    last, (weight, first, second) = lax.optimization_barrier((last, new))
    act_grad = last.reshape(SIDE * LANES, ROWS)
    return (weight.T, first.T, second.T, act_grad)


def solution(mesh):
    grid = Mesh(mesh.devices.reshape(SIDE, SIDE, SPLITS // 2, 2), ("z", "y", "x", "c"))
    dp, mp = ("z", "y"), ("x", "c")
    return jax.shard_map(
        shards,
        mesh=grid,
        in_specs=(P(dp, mp), P(dp, mp), P(dp, mp), P(), P(dp + mp, None), P(dp, mp)),
        out_specs=(P(dp, mp), P(dp, mp), P(dp, mp), P(mp, dp)),
        check_vma=False,
    )
```

```python
import jax
import jax.numpy as jnp
from jax import lax
from jax.experimental import pallas as pl
from jax.experimental.pallas import tpu as pltpu
from jax.sharding import Mesh
from jax.sharding import PartitionSpec as P

D = 8192
STEP = 24
SHARDS = 24
CAP = 384
ROWS = 128
COLS = 448
GROUPS = 64
SPLITS = 8
TOKENS = 16
SIDE = 8
STRIPS = COLS // 8
LANES = 128

beta_one = 0.9
beta_two = 0.95
epsilon = 1e-08
learn_rate = 0.05
decay_rate = 0.2

f32 = jnp.float32
bf16 = jnp.bfloat16
PARAMS = pltpu.CompilerParams(vmem_limit_bytes=48 * 1024 * 1024)


def pack_kernel(weight_ref, first_ref, second_ref, out_ref):
    held = [r[...].astype(f32) for r in (weight_ref, first_ref, second_ref)]
    for s in range(STRIPS):
        tiles = [
            t[s * 8 : s * 8 + 8, q * LANES : (q + 1) * LANES]
            for q in range(CAP // LANES)
            for t in held
        ]
        out_ref[s] = jnp.concatenate(tiles, axis=0).astype(bf16)
    out_ref[STRIPS:] = jnp.zeros((GROUPS - STRIPS, 72, LANES), bf16)


def pack(weight, first, second):
    return pl.pallas_call(
        pack_kernel,
        out_shape=jax.ShapeDtypeStruct((GROUPS, 72, LANES), bf16),
        compiler_params=PARAMS,
        name="pack",
    )(weight, first, second)


def place_kernel(offsets_ref, slots_ref, out_ref, rows_ref):
    lane = lax.broadcasted_iota(jnp.int32, (24, LANES), 1)
    for k in range(SHARDS):
        begin = offsets_ref[k]
        block = begin // LANES
        shift = begin % LANES
        turned = pltpu.roll(slots_ref[k].astype(f32), shift, 1).reshape(3, 24, LANES)
        rows_ref[block] = jnp.where(lane >= shift, turned[0], rows_ref[block])
        rows_ref[block + 1] = jnp.where(lane >= shift, turned[1], turned[0])
        rows_ref[block + 2] = jnp.where(lane >= shift, turned[2], turned[1])
        rows_ref[block + 3] = turned[2]
    for z in range(SIDE):
        rows = rows_ref[z * SIDE : (z + 1) * SIDE]
        weights = rows[:, :8].reshape(64, LANES).astype(bf16)
        for y in range(SIDE):
            out_ref[z * SIDE + y, :64] = weights
            out_ref[z * SIDE + y, 64:] = rows[y, 8:].astype(bf16)


def place(offsets, slots):
    return pl.pallas_call(
        place_kernel,
        in_specs=[
            pl.BlockSpec(memory_space=pltpu.SMEM),
            pl.BlockSpec(memory_space=pltpu.VMEM),
        ],
        out_shape=jax.ShapeDtypeStruct((GROUPS, 80, LANES), bf16),
        scratch_shapes=[pltpu.VMEM((GROUPS + 4, 24, LANES), f32)],
        compiler_params=PARAMS,
        name="place",
    )(offsets, slots)


def send_kernel(place_ref, act_ref, *out_refs):
    for s, out_ref in enumerate(out_refs):
        z = lax.rem(place_ref[0] + s, SIDE)
        for y in range(SIDE):
            at = pl.multiple_of((z * SIDE + y) * LANES, LANES)
            out_ref[y * TOKENS : (y + 1) * TOKENS] = act_ref[:, pl.ds(at, LANES)]


def send_blocks(place, act):
    return pl.pallas_call(
        send_kernel,
        in_specs=[
            pl.BlockSpec(memory_space=pltpu.SMEM),
            pl.BlockSpec(memory_space=pltpu.VMEM),
        ],
        out_shape=[jax.ShapeDtypeStruct((SIDE * TOKENS, LANES), bf16)] * SIDE,
        compiler_params=PARAMS,
        name="send_blocks",
    )(place, act)


def sums_kernel(place_ref, own_ref, other_ref, up_ref, out_ref):
    core = place_ref[3]
    halves = []
    for c in (core, 1 - core):
        halves.append(jnp.concatenate([up_ref[2 * x + core, c] for x in range(4)], axis=1))
    up = jnp.concatenate(halves, axis=0)
    own = own_ref[...].astype(f32)
    other = other_ref[...].astype(f32)
    for y in range(SIDE):
        weight = jnp.concatenate(
            [w[:, y * 8 : y * 8 + 8].reshape(COLS, ROWS) for w in (own, other)], axis=0
        )
        sums = jnp.dot(weight.T.astype(bf16), up, preferred_element_type=f32).astype(bf16)
        for x in range(4):
            out_ref[x, y] = sums[:, x * LANES : (x + 1) * LANES]


def act_sums(place, own, other, up):
    vmem = pl.BlockSpec(memory_space=pltpu.VMEM)
    return pl.pallas_call(
        sums_kernel,
        in_specs=[pl.BlockSpec(memory_space=pltpu.SMEM)] + [vmem] * 3,
        out_shape=jax.ShapeDtypeStruct((SPLITS // 2, SIDE, ROWS, LANES), bf16),
        compiler_params=PARAMS,
        name="act_sums",
    )(place, own, other, up)


def total_kernel(parts_ref, out_ref):
    for y in range(SIDE):
        total = parts_ref[0, y].astype(f32)
        for x in range(1, SPLITS // 2):
            total = total + parts_ref[x, y].astype(f32)
        out_ref[y] = total.T.astype(bf16)


def act_total(parts):
    return pl.pallas_call(
        total_kernel,
        out_shape=jax.ShapeDtypeStruct((SIDE, LANES, ROWS), bf16),
        compiler_params=PARAMS,
        name="act_total",
    )(parts)


def grad_kernel(place_ref, own_ref, other_ref, up_ref, out_ref):
    up = jnp.concatenate([up_ref[z, place_ref[3]] for z in range(SIDE)], axis=1)
    for y in range(0, SIDE, 2):
        act = []
        for rows in (slice(y * TOKENS, (y + 1) * TOKENS), slice((y + 1) * TOKENS, (y + 2) * TOKENS)):
            tiles = []
            for z in range(SIDE):
                back = lax.rem(place_ref[0] + SIDE - z, SIDE)
                for m in range(SPLITS):
                    x = lax.rem(place_ref[2] + 4 - m // 2, 4)
                    same = place_ref[3] == m % 2
                    tiles.append(jnp.where(same, own_ref[x, back, rows], other_ref[x, back, rows]))
            act.append(jnp.concatenate(tiles, axis=0))
        part = jnp.dot(up, jnp.concatenate(act, axis=1), preferred_element_type=f32)
        out_ref[y] = part[:, :LANES]
        out_ref[y + 1] = part[:, LANES:]


def grad_parts(place, own, other, up):
    vmem = pl.BlockSpec(memory_space=pltpu.VMEM)
    return pl.pallas_call(
        grad_kernel,
        in_specs=[pl.BlockSpec(memory_space=pltpu.SMEM)] + [vmem] * 3,
        out_shape=jax.ShapeDtypeStruct((SIDE, COLS, ROWS), f32),
        compiler_params=PARAMS,
        name="grad_parts",
    )(place, own, other, up)


def adamw_update(weight, moment_one, moment_two, gradient):
    first_new = beta_one * moment_one + (1.0 - beta_one) * gradient
    second_new = beta_two * moment_two + (1.0 - beta_two) * gradient * gradient
    first_hat = first_new / (1.0 - beta_one**STEP)
    second_hat = second_new / (1.0 - beta_two**STEP)
    weight_new = weight - learn_rate * (
        first_hat / (jnp.sqrt(second_hat) + epsilon) + decay_rate * weight
    )
    return (weight_new, first_new, second_new)


def update_kernel(place_ref, state_ref, grad_ref, weight_ref, first_ref, second_ref):
    mine = place_ref[1]
    state = state_ref[:STRIPS].astype(f32)
    weight = state[:, :8]
    for y in range(1, SIDE):
        weight = jnp.where(mine == y, state[:, y * 8 : y * 8 + 8], weight)
    old = [t.reshape(COLS, ROWS) for t in (weight, state[:, 64:72], state[:, 72:])]
    new = adamw_update(old[0], old[1], old[2], grad_ref[...])
    for ref, value in zip((weight_ref, first_ref, second_ref), new):
        ref[...] = value


def update(place, state, grad):
    out = jax.ShapeDtypeStruct((COLS, ROWS), f32)
    return pl.pallas_call(
        update_kernel,
        in_specs=[
            pl.BlockSpec(memory_space=pltpu.SMEM),
            pl.BlockSpec(memory_space=pltpu.VMEM),
            pl.BlockSpec(memory_space=pltpu.VMEM),
        ],
        out_shape=[out, out, out],
        compiler_params=PARAMS,
        name="update",
    )(place, state, grad)


def exchange(x, axis):
    return lax.all_to_all(x, axis, split_axis=0, concat_axis=0, tiled=True)


def shift(x, axis, by):
    n = lax.axis_size(axis)
    return lax.ppermute(x, axis, [(i, (i + by) % n) for i in range(n)])


def shards(old_weight, old_first, old_second, old_offsets, activations, upstream):
    here = jnp.stack([lax.axis_index(a) for a in ("z", "y", "x", "c")])
    up = lax.all_gather(upstream.T, ("z", "c"), axis=0).reshape(SIDE, 2, COLS, LANES)
    halves = [t.T.astype(bf16) for t in (old_weight, old_first, old_second)]
    got = exchange(pack(*halves), ("z", "y"))
    sent = send_blocks(here, activations)
    act = jnp.stack([sent[0]] + [shift(sent[s], "z", s) for s in range(1, SIDE)])
    got, act = lax.optimization_barrier((got, act))
    own = jnp.stack([act] + [shift(act, "x", s) for s in range(1, SPLITS // 2)])
    own, up = lax.optimization_barrier((own, up))
    state = exchange(place(old_offsets, got), ("z", "y"))
    parts = grad_parts(here, own, shift(own, "c", 1), up)
    state, parts = lax.optimization_barrier((state, parts))
    grad = lax.psum_scatter(parts, "y", scatter_dimension=0)
    weight = state[:STRIPS, : SIDE * 8]
    sums = act_sums(here, weight, shift(weight, "c", 1), up)
    total = act_total(exchange(sums, "x"))
    last = exchange(total, "y")
    new = update(here, state, grad)
    last, (weight, first, second) = lax.optimization_barrier((last, new))
    act_grad = last.reshape(SIDE * LANES, ROWS)
    return (weight.T, first.T, second.T, act_grad)


def solution(mesh):
    grid = Mesh(mesh.devices.reshape(SIDE, SIDE, SPLITS // 2, 2), ("z", "y", "x", "c"))
    dp, mp = ("z", "y"), ("x", "c")
    return jax.shard_map(
        shards,
        mesh=grid,
        in_specs=(P(dp, mp), P(dp, mp), P(dp, mp), P(), P(dp + mp, None), P(dp, mp)),
        out_specs=(P(dp, mp), P(dp, mp), P(dp, mp), P(mp, dp)),
        check_vma=False,
    )
```

```python
import jax
import jax.numpy as jnp
from jax import lax
from jax.experimental import pallas as pl
from jax.experimental.pallas import tpu as pltpu
from jax.sharding import Mesh
from jax.sharding import PartitionSpec as P

D = 8192
STEP = 24
SHARDS = 24
CAP = 384
ROWS = 128
COLS = 448
GROUPS = 64
SPLITS = 8
TOKENS = 16
SIDE = 8
STRIPS = COLS // 8
LANES = 128

beta_one = 0.9
beta_two = 0.95
epsilon = 1e-08
learn_rate = 0.05
decay_rate = 0.2

f32 = jnp.float32
bf16 = jnp.bfloat16
PARAMS = pltpu.CompilerParams(vmem_limit_bytes=48 * 1024 * 1024)


def pack_kernel(weight_ref, first_ref, second_ref, out_ref):
    held = [r[...].astype(f32) for r in (weight_ref, first_ref, second_ref)]
    for s in range(STRIPS):
        tiles = [
            t[s * 8 : s * 8 + 8, q * LANES : (q + 1) * LANES]
            for q in range(CAP // LANES)
            for t in held
        ]
        out_ref[s] = jnp.concatenate(tiles, axis=0).astype(bf16)
    out_ref[STRIPS:] = jnp.zeros((GROUPS - STRIPS, 72, LANES), bf16)


def pack(weight, first, second):
    return pl.pallas_call(
        pack_kernel,
        out_shape=jax.ShapeDtypeStruct((GROUPS, 72, LANES), bf16),
        compiler_params=PARAMS,
        name="pack",
    )(weight, first, second)


def place_kernel(offsets_ref, slots_ref, out_ref, rows_ref):
    lane = lax.broadcasted_iota(jnp.int32, (24, LANES), 1)
    for k in range(SHARDS):
        begin = offsets_ref[k]
        block = begin // LANES
        shift = begin % LANES
        turned = pltpu.roll(slots_ref[k].astype(f32), shift, 1).reshape(3, 24, LANES)
        rows_ref[block] = jnp.where(lane >= shift, turned[0], rows_ref[block])
        rows_ref[block + 1] = jnp.where(lane >= shift, turned[1], turned[0])
        rows_ref[block + 2] = jnp.where(lane >= shift, turned[2], turned[1])
        rows_ref[block + 3] = turned[2]
    for z in range(SIDE):
        rows = rows_ref[z * SIDE : (z + 1) * SIDE]
        weights = rows[:, :8].reshape(64, LANES).astype(bf16)
        for y in range(SIDE):
            out_ref[z * SIDE + y, :64] = weights
            out_ref[z * SIDE + y, 64:] = rows[y, 8:].astype(bf16)


def place(offsets, slots):
    return pl.pallas_call(
        place_kernel,
        in_specs=[
            pl.BlockSpec(memory_space=pltpu.SMEM),
            pl.BlockSpec(memory_space=pltpu.VMEM),
        ],
        out_shape=jax.ShapeDtypeStruct((GROUPS, 80, LANES), bf16),
        scratch_shapes=[pltpu.VMEM((GROUPS + 4, 24, LANES), f32)],
        compiler_params=PARAMS,
        name="place",
    )(offsets, slots)


def send_kernel(place_ref, act_ref, *out_refs):
    for s, out_ref in enumerate(out_refs):
        z = lax.rem(place_ref[0] + s, SIDE)
        for y in range(SIDE):
            at = pl.multiple_of((z * SIDE + y) * LANES, LANES)
            out_ref[y * TOKENS : (y + 1) * TOKENS] = act_ref[:, pl.ds(at, LANES)]


def send_blocks(place, act):
    return pl.pallas_call(
        send_kernel,
        in_specs=[
            pl.BlockSpec(memory_space=pltpu.SMEM),
            pl.BlockSpec(memory_space=pltpu.VMEM),
        ],
        out_shape=[jax.ShapeDtypeStruct((SIDE * TOKENS, LANES), bf16)] * SIDE,
        compiler_params=PARAMS,
        name="send_blocks",
    )(place, act)


def sums_kernel(place_ref, own_ref, other_ref, up_ref, out_ref):
    core = place_ref[3]
    halves = []
    for c in (core, 1 - core):
        halves.append(jnp.concatenate([up_ref[2 * x + core, c] for x in range(4)], axis=1))
    up = jnp.concatenate(halves, axis=0)
    own = own_ref[...].astype(f32)
    other = other_ref[...].astype(f32)
    for y in range(SIDE):
        weight = jnp.concatenate(
            [w[:, y * 8 : y * 8 + 8].reshape(COLS, ROWS) for w in (own, other)], axis=0
        )
        sums = jnp.dot(weight.T.astype(bf16), up, preferred_element_type=f32).astype(bf16)
        for x in range(4):
            out_ref[x, y] = sums[:, x * LANES : (x + 1) * LANES]


def act_sums(place, own, other, up):
    vmem = pl.BlockSpec(memory_space=pltpu.VMEM)
    return pl.pallas_call(
        sums_kernel,
        in_specs=[pl.BlockSpec(memory_space=pltpu.SMEM)] + [vmem] * 3,
        out_shape=jax.ShapeDtypeStruct((SPLITS // 2, SIDE, ROWS, LANES), bf16),
        compiler_params=PARAMS,
        name="act_sums",
    )(place, own, other, up)


def total_kernel(parts_ref, out_ref):
    for y in range(SIDE):
        total = parts_ref[0, y].astype(f32)
        for x in range(1, SPLITS // 2):
            total = total + parts_ref[x, y].astype(f32)
        out_ref[y] = total.T.astype(bf16)


def act_total(parts):
    return pl.pallas_call(
        total_kernel,
        out_shape=jax.ShapeDtypeStruct((SIDE, LANES, ROWS), bf16),
        compiler_params=PARAMS,
        name="act_total",
    )(parts)


def grad_kernel(place_ref, own_ref, other_ref, up_ref, out_ref):
    up = jnp.concatenate([up_ref[z, place_ref[3]] for z in range(SIDE)], axis=1)
    for y in range(0, SIDE, 2):
        act = []
        for rows in (slice(y * TOKENS, (y + 1) * TOKENS), slice((y + 1) * TOKENS, (y + 2) * TOKENS)):
            tiles = []
            for z in range(SIDE):
                back = lax.rem(place_ref[0] + SIDE - z, SIDE)
                for m in range(SPLITS):
                    x = lax.rem(place_ref[2] + 4 - m // 2, 4)
                    same = place_ref[3] == m % 2
                    tiles.append(jnp.where(same, own_ref[x, back, rows], other_ref[x, back, rows]))
            act.append(jnp.concatenate(tiles, axis=0))
        part = jnp.dot(up, jnp.concatenate(act, axis=1), preferred_element_type=f32)
        out_ref[y] = part[:, :LANES]
        out_ref[y + 1] = part[:, LANES:]


def grad_parts(place, own, other, up):
    vmem = pl.BlockSpec(memory_space=pltpu.VMEM)
    return pl.pallas_call(
        grad_kernel,
        in_specs=[pl.BlockSpec(memory_space=pltpu.SMEM)] + [vmem] * 3,
        out_shape=jax.ShapeDtypeStruct((SIDE, COLS, ROWS), f32),
        compiler_params=PARAMS,
        name="grad_parts",
    )(place, own, other, up)


def adamw_update(weight, moment_one, moment_two, gradient):
    first_new = beta_one * moment_one + (1.0 - beta_one) * gradient
    second_new = beta_two * moment_two + (1.0 - beta_two) * gradient * gradient
    first_hat = first_new / (1.0 - beta_one**STEP)
    second_hat = second_new / (1.0 - beta_two**STEP)
    weight_new = weight - learn_rate * (
        first_hat / (jnp.sqrt(second_hat) + epsilon) + decay_rate * weight
    )
    return (weight_new, first_new, second_new)


def update_kernel(place_ref, state_ref, grad_ref, weight_ref, first_ref, second_ref):
    mine = place_ref[1]
    state = state_ref[:STRIPS].astype(f32)
    weight = state[:, :8]
    for y in range(1, SIDE):
        weight = jnp.where(mine == y, state[:, y * 8 : y * 8 + 8], weight)
    old = [t.reshape(COLS, ROWS) for t in (weight, state[:, 64:72], state[:, 72:])]
    new = adamw_update(old[0], old[1], old[2], grad_ref[...])
    for ref, value in zip((weight_ref, first_ref, second_ref), new):
        ref[...] = value


def update(place, state, grad):
    out = jax.ShapeDtypeStruct((COLS, ROWS), f32)
    return pl.pallas_call(
        update_kernel,
        in_specs=[
            pl.BlockSpec(memory_space=pltpu.SMEM),
            pl.BlockSpec(memory_space=pltpu.VMEM),
            pl.BlockSpec(memory_space=pltpu.VMEM),
        ],
        out_shape=[out, out, out],
        compiler_params=PARAMS,
        name="update",
    )(place, state, grad)


def exchange(x, axis):
    return lax.all_to_all(x, axis, split_axis=0, concat_axis=0, tiled=True)


def shift(x, axis, by):
    n = lax.axis_size(axis)
    return lax.ppermute(x, axis, [(i, (i + by) % n) for i in range(n)])


def shards(old_weight, old_first, old_second, old_offsets, activations, upstream):
    here = jnp.stack([lax.axis_index(a) for a in ("z", "y", "x", "c")])
    up = lax.all_gather(upstream.T, ("z", "c"), axis=0).reshape(SIDE, 2, COLS, LANES)
    blocks = pack(old_weight.T, old_first.T.astype(bf16), old_second.T.astype(bf16))
    got = exchange(blocks, ("z", "y"))
    sent = send_blocks(here, activations)
    act = jnp.stack([sent[0]] + [shift(sent[s], "z", s) for s in range(1, SIDE)])
    got, act = lax.optimization_barrier((got, act))
    own = jnp.stack([act] + [shift(act, "x", s) for s in range(1, SPLITS // 2)])
    own, up = lax.optimization_barrier((own, up))
    state = exchange(place(old_offsets, got), ("z", "y"))
    parts = grad_parts(here, own, shift(own, "c", 1), up)
    state, parts = lax.optimization_barrier((state, parts))
    grad = lax.psum_scatter(parts, "y", scatter_dimension=0)
    weight = state[:STRIPS, : SIDE * 8]
    sums = act_sums(here, weight, shift(weight, "c", 1), up)
    total = act_total(exchange(sums, "x"))
    last = exchange(total, "y")
    new = update(here, state, grad)
    last, (weight, first, second) = lax.optimization_barrier((last, new))
    act_grad = last.reshape(SIDE * LANES, ROWS)
    return (weight.T, first.T, second.T, act_grad)


def solution(mesh):
    grid = Mesh(mesh.devices.reshape(SIDE, SIDE, SPLITS // 2, 2), ("z", "y", "x", "c"))
    dp, mp = ("z", "y"), ("x", "c")
    return jax.shard_map(
        shards,
        mesh=grid,
        in_specs=(P(dp, mp), P(dp, mp), P(dp, mp), P(), P(dp + mp, None), P(dp, mp)),
        out_specs=(P(dp, mp), P(dp, mp), P(dp, mp), P(mp, dp)),
        check_vma=False,
    )
```

```python
import jax
import jax.numpy as jnp
from jax import lax
from jax.experimental import pallas as pl
from jax.experimental.pallas import tpu as pltpu
from jax.sharding import Mesh
from jax.sharding import PartitionSpec as P

D = 8192
STEP = 24
SHARDS = 24
CAP = 384
ROWS = 128
COLS = 448
GROUPS = 64
SPLITS = 8
TOKENS = 16
SIDE = 8
STRIPS = COLS // 8
LANES = 128

beta_one = 0.9
beta_two = 0.95
epsilon = 1e-08
learn_rate = 0.05
decay_rate = 0.2

f32 = jnp.float32
bf16 = jnp.bfloat16
PARAMS = pltpu.CompilerParams(vmem_limit_bytes=48 * 1024 * 1024)


def pack_kernel(weight_ref, first_ref, second_ref, out_ref):
    held = [r[...].astype(f32) for r in (weight_ref, first_ref, second_ref)]
    for s in range(STRIPS):
        tiles = [
            t[s * 8 : s * 8 + 8, q * LANES : (q + 1) * LANES]
            for q in range(CAP // LANES)
            for t in held
        ]
        out_ref[s] = jnp.concatenate(tiles, axis=0).astype(bf16)
    out_ref[STRIPS:] = jnp.zeros((GROUPS - STRIPS, 72, LANES), bf16)


def pack(weight, first, second):
    return pl.pallas_call(
        pack_kernel,
        out_shape=jax.ShapeDtypeStruct((GROUPS, 72, LANES), bf16),
        compiler_params=PARAMS,
        name="pack",
    )(weight, first, second)


def place_kernel(offsets_ref, slots_ref, out_ref, rows_ref):
    lane = lax.broadcasted_iota(jnp.int32, (24, LANES), 1)
    begins = [offsets_ref[k] for k in range(SHARDS)]
    rolled = [
        pltpu.roll(slots_ref[k].astype(f32), begin % LANES, 1) for k, begin in enumerate(begins)
    ]
    for begin, turned in zip(begins, rolled):
        block = begin // LANES
        shift = begin % LANES
        turned = turned.reshape(3, 24, LANES)
        rows_ref[block] = jnp.where(lane >= shift, turned[0], rows_ref[block])
        rows_ref[block + 1] = jnp.where(lane >= shift, turned[1], turned[0])
        rows_ref[block + 2] = jnp.where(lane >= shift, turned[2], turned[1])
        rows_ref[block + 3] = turned[2]
    for z in range(SIDE):
        rows = rows_ref[z * SIDE : (z + 1) * SIDE]
        weights = rows[:, :8].reshape(64, LANES).astype(bf16)
        for y in range(SIDE):
            out_ref[z * SIDE + y, :64] = weights
            out_ref[z * SIDE + y, 64:] = rows[y, 8:].astype(bf16)


def place(offsets, slots):
    return pl.pallas_call(
        place_kernel,
        in_specs=[
            pl.BlockSpec(memory_space=pltpu.SMEM),
            pl.BlockSpec(memory_space=pltpu.VMEM),
        ],
        out_shape=jax.ShapeDtypeStruct((GROUPS, 80, LANES), bf16),
        scratch_shapes=[pltpu.VMEM((GROUPS + 4, 24, LANES), f32)],
        compiler_params=PARAMS,
        name="place",
    )(offsets, slots)


def send_kernel(place_ref, act_ref, *out_refs):
    for s, out_ref in enumerate(out_refs):
        z = lax.rem(place_ref[0] + s, SIDE)
        for y in range(SIDE):
            at = pl.multiple_of((z * SIDE + y) * LANES, LANES)
            out_ref[y * TOKENS : (y + 1) * TOKENS] = act_ref[:, pl.ds(at, LANES)]


def send_blocks(place, act):
    return pl.pallas_call(
        send_kernel,
        in_specs=[
            pl.BlockSpec(memory_space=pltpu.SMEM),
            pl.BlockSpec(memory_space=pltpu.VMEM),
        ],
        out_shape=[jax.ShapeDtypeStruct((SIDE * TOKENS, LANES), bf16)] * SIDE,
        compiler_params=PARAMS,
        name="send_blocks",
    )(place, act)


def sums_kernel(place_ref, own_ref, other_ref, up_ref, out_ref):
    core = place_ref[3]
    halves = []
    for c in (core, 1 - core):
        halves.append(jnp.concatenate([up_ref[2 * x + core, c] for x in range(4)], axis=1))
    up = jnp.concatenate(halves, axis=0)
    own = own_ref[...].astype(f32)
    other = other_ref[...].astype(f32)
    for y in range(SIDE):
        weight = jnp.concatenate(
            [w[:, y * 8 : y * 8 + 8].reshape(COLS, ROWS) for w in (own, other)], axis=0
        )
        sums = jnp.dot(weight.T.astype(bf16), up, preferred_element_type=f32).astype(bf16)
        for x in range(4):
            out_ref[x, y] = sums[:, x * LANES : (x + 1) * LANES]


def act_sums(place, own, other, up):
    vmem = pl.BlockSpec(memory_space=pltpu.VMEM)
    return pl.pallas_call(
        sums_kernel,
        in_specs=[pl.BlockSpec(memory_space=pltpu.SMEM)] + [vmem] * 3,
        out_shape=jax.ShapeDtypeStruct((SPLITS // 2, SIDE, ROWS, LANES), bf16),
        compiler_params=PARAMS,
        name="act_sums",
    )(place, own, other, up)


def total_kernel(parts_ref, out_ref):
    for y in range(SIDE):
        total = parts_ref[0, y].astype(f32)
        for x in range(1, SPLITS // 2):
            total = total + parts_ref[x, y].astype(f32)
        out_ref[y] = total.T.astype(bf16)


def act_total(parts):
    return pl.pallas_call(
        total_kernel,
        out_shape=jax.ShapeDtypeStruct((SIDE, LANES, ROWS), bf16),
        compiler_params=PARAMS,
        name="act_total",
    )(parts)


def grad_kernel(place_ref, own_ref, other_ref, up_ref, out_ref):
    up = jnp.concatenate([up_ref[z, place_ref[3]] for z in range(SIDE)], axis=1)
    for y in range(0, SIDE, 2):
        act = []
        for rows in (slice(y * TOKENS, (y + 1) * TOKENS), slice((y + 1) * TOKENS, (y + 2) * TOKENS)):
            tiles = []
            for z in range(SIDE):
                back = lax.rem(place_ref[0] + SIDE - z, SIDE)
                for m in range(SPLITS):
                    x = lax.rem(place_ref[2] + 4 - m // 2, 4)
                    same = place_ref[3] == m % 2
                    tiles.append(jnp.where(same, own_ref[x, back, rows], other_ref[x, back, rows]))
            act.append(jnp.concatenate(tiles, axis=0))
        part = jnp.dot(up, jnp.concatenate(act, axis=1), preferred_element_type=f32)
        out_ref[y] = part[:, :LANES]
        out_ref[y + 1] = part[:, LANES:]


def grad_parts(place, own, other, up):
    vmem = pl.BlockSpec(memory_space=pltpu.VMEM)
    return pl.pallas_call(
        grad_kernel,
        in_specs=[pl.BlockSpec(memory_space=pltpu.SMEM)] + [vmem] * 3,
        out_shape=jax.ShapeDtypeStruct((SIDE, COLS, ROWS), f32),
        compiler_params=PARAMS,
        name="grad_parts",
    )(place, own, other, up)


def adamw_update(weight, moment_one, moment_two, gradient):
    first_new = beta_one * moment_one + (1.0 - beta_one) * gradient
    second_new = beta_two * moment_two + (1.0 - beta_two) * gradient * gradient
    first_hat = first_new / (1.0 - beta_one**STEP)
    second_hat = second_new / (1.0 - beta_two**STEP)
    weight_new = weight - learn_rate * (
        first_hat / (jnp.sqrt(second_hat) + epsilon) + decay_rate * weight
    )
    return (weight_new, first_new, second_new)


def update_kernel(place_ref, state_ref, grad_ref, weight_ref, first_ref, second_ref):
    mine = place_ref[1]
    state = state_ref[:STRIPS].astype(f32)
    weight = state[:, :8]
    for y in range(1, SIDE):
        weight = jnp.where(mine == y, state[:, y * 8 : y * 8 + 8], weight)
    old = [t.reshape(COLS, ROWS) for t in (weight, state[:, 64:72], state[:, 72:])]
    new = adamw_update(old[0], old[1], old[2], grad_ref[...])
    for ref, value in zip((weight_ref, first_ref, second_ref), new):
        ref[...] = value


def update(place, state, grad):
    out = jax.ShapeDtypeStruct((COLS, ROWS), f32)
    return pl.pallas_call(
        update_kernel,
        in_specs=[
            pl.BlockSpec(memory_space=pltpu.SMEM),
            pl.BlockSpec(memory_space=pltpu.VMEM),
            pl.BlockSpec(memory_space=pltpu.VMEM),
        ],
        out_shape=[out, out, out],
        compiler_params=PARAMS,
        name="update",
    )(place, state, grad)


def exchange(x, axis):
    return lax.all_to_all(x, axis, split_axis=0, concat_axis=0, tiled=True)


def shift(x, axis, by):
    n = lax.axis_size(axis)
    return lax.ppermute(x, axis, [(i, (i + by) % n) for i in range(n)])


def shards(old_weight, old_first, old_second, old_offsets, activations, upstream):
    here = jnp.stack([lax.axis_index(a) for a in ("z", "y", "x", "c")])
    up = lax.all_gather(upstream.T, ("z", "c"), axis=0).reshape(SIDE, 2, COLS, LANES)
    blocks = pack(old_weight.T, old_first.T.astype(bf16), old_second.T.astype(bf16))
    got = exchange(blocks, ("z", "y"))
    sent = send_blocks(here, activations)
    act = jnp.stack([sent[0]] + [shift(sent[s], "z", s) for s in range(1, SIDE)])
    got, act = lax.optimization_barrier((got, act))
    own = jnp.stack([act] + [shift(act, "x", s) for s in range(1, SPLITS // 2)])
    own, up = lax.optimization_barrier((own, up))
    state = exchange(place(old_offsets, got), ("z", "y"))
    parts = grad_parts(here, own, shift(own, "c", 1), up)
    state, parts = lax.optimization_barrier((state, parts))
    grad = lax.psum_scatter(parts, "y", scatter_dimension=0)
    weight = state[:STRIPS, : SIDE * 8]
    sums = act_sums(here, weight, shift(weight, "c", 1), up)
    total = act_total(exchange(sums, "x"))
    last = exchange(total, "y")
    new = update(here, state, grad)
    last, (weight, first, second) = lax.optimization_barrier((last, new))
    act_grad = last.reshape(SIDE * LANES, ROWS)
    return (weight.T, first.T, second.T, act_grad)


def solution(mesh):
    grid = Mesh(mesh.devices.reshape(SIDE, SIDE, SPLITS // 2, 2), ("z", "y", "x", "c"))
    dp, mp = ("z", "y"), ("x", "c")
    return jax.shard_map(
        shards,
        mesh=grid,
        in_specs=(P(dp, mp), P(dp, mp), P(dp, mp), P(), P(dp + mp, None), P(dp, mp)),
        out_specs=(P(dp, mp), P(dp, mp), P(dp, mp), P(mp, dp)),
        check_vma=False,
    )
```
